512 devices in a mesh: tm: 64 (over x, z), mp: 8 (over y, core).
Axes of the slice: x: 4, y: 4, z: 16, core: 2. Of those that a mesh axis runs over, the one named last changes fastest.
Arguments:
- mel_frames: bfloat16 [38400, 128], P('tm'), may hold values from -6 to 6
- conv_weight: bfloat16 [384, 1280], P(None, 'mp'), may hold values from -0.3125 to 0.3125
- patches: bfloat16 [49152, 1280], P('tm', 'mp'), may hold values from -6 to 6
- vit_up: bfloat16 [1280, 5120], P(None, 'mp'), may hold values from -0.15625 to 0.15625
- vit_down: bfloat16 [5120, 1280], P('mp'), may hold values from -0.078125 to 0.078125
- audio_proj: bfloat16 [1280, 3584], P('tm', 'mp'), may hold values from -0.15625 to 0.15625
- merger: bfloat16 [5120, 3584], P('tm', 'mp'), may hold values from -0.078125 to 0.078125
- text_rows: bfloat16 [512, 64, 3584], P(None, 'tm', 'mp'), may hold values from -6 to 6
- span_order: int32 [192], replicated, may hold values from 0 to 191, as said below
- offsets: int32 [192], replicated, may hold values from 0 to 32726, as said below
- audio_count: int32 [192], replicated, may hold values from 10 to 50
- video_count: int32 [192], replicated, may hold values from 32 to 64
Outputs:
- sequence_rows: bfloat16 [512, 64, 3584], P(None, 'tm', 'mp')
The draws below stay inside these ranges and needn't reach their ends.
Inputs may be any that keep to these rules, and one draw needn't show every extreme that they name: span_order lists each span once. Listed spans take increasing, non-intersecting ranges of video_count + audio_count positions starting at offsets, all before 32768.
All inputs are finite; a program needn't handle non-finite values.
Results may differ from the reference program's by a relative error of at most 0.0034.
Values may be sent and summed in bfloat16 or wider, within the bound.
No kernel may reach another device: no remote copies, remote signals or barrier semaphores. Data moves between devices by JAX's collectives and lax.ppermute only.
A program may use at most 64 MiB of HBM per device.

```python
import jax
import jax.numpy as jnp
from jax import lax

DA = 1280
MEL = 128
DV = 1280
FFV = 5120
DL = 3584
AT = 50
VT = 64
SEQ_DEV = 512
OWNERS = 64
NCH = 192
SEQ = 32768
MEL_ROWS = 38400
PATCHES = 49152


def layout(key):
    audio = jax.random.randint(jax.random.fold_in(key, 11), (NCH,), AT // 5, AT + 1).astype(jnp.int32)
    video = jax.random.randint(jax.random.fold_in(key, 12), (NCH,), VT // 2, VT + 1).astype(jnp.int32)
    chosen = jax.random.randint(jax.random.fold_in(key, 13), (), 0, NCH).astype(jnp.int32)
    offset_pick = jax.random.randint(jax.random.fold_in(key, 14), (), 1, NCH).astype(jnp.int32)
    lowest = (chosen + offset_pick) % NCH
    audio = audio.at[lowest].set(AT // 5).at[chosen].set(AT)
    video = video.at[lowest].set(VT // 2).at[chosen].set(VT)
    listing = jax.random.permutation(jax.random.fold_in(key, 15), NCH).astype(jnp.int32)
    where_low = jnp.argmax((listing == lowest).astype(jnp.int32)).astype(jnp.int32)
    final_entry = listing[NCH - 1]
    listing = listing.at[where_low].set(final_entry).at[NCH - 1].set(lowest)
    lengths = (audio + video)[listing]
    text_count = SEQ - jnp.sum(lengths)
    weights = jax.random.randint(jax.random.fold_in(key, 16), (NCH,), 1, 17).astype(jnp.int32)
    climbing = jnp.cumsum(weights).astype(jnp.int32)
    rising = climbing - climbing[0]
    bounds = text_count * rising // rising[NCH - 1]
    starts = bounds + jnp.cumsum(lengths).astype(jnp.int32) - lengths
    return (listing, starts.astype(jnp.int32), audio, video)


def draw_span_order(key, part):
    shared = layout(key)
    return shared[0].astype(jnp.int32)


def draw_offsets(key, part):
    shared = layout(key)
    return shared[1].astype(jnp.int32)


def draw_audio_count(key, part):
    shared = layout(key)
    return shared[2].astype(jnp.int32)


def draw_video_count(key, part):
    shared = layout(key)
    return shared[3].astype(jnp.int32)


def block_levels(rng, extent, shards, low, top_value):
    factor_of = 1.0
    for dim, blocks in shards:
        steps = jax.random.uniform(jax.random.fold_in(jax.random.fold_in(rng, 6), dim), (blocks,), jnp.float32, low / len(shards), top_value / len(shards))
        factor_of = factor_of * jnp.repeat(jnp.exp(steps), extent[dim] // blocks).reshape((-1,) + (1,) * (len(extent) - 1 - dim))
    return factor_of


def scatter_about(stream_key, dims, scale, bound, pieces=(), kind=jnp.bfloat16):
    entries = scale * jax.random.normal(stream_key, dims, jnp.float32)
    if pieces:
        entries = entries * block_levels(stream_key, dims, pieces, -0.22, 0.18)
    return jnp.clip(entries, -bound, bound).astype(kind)


def setup_inputs(seed: int = 0) -> dict:
    arg_keys = jax.random.split(jax.random.key(seed), 13)
    mel_frames = scatter_about(arg_keys[0], (MEL_ROWS, MEL), 1.0, 6.0, ((0, 64),))
    conv_weight = scatter_about(arg_keys[1], (3 * MEL, DA), (3 * MEL) ** -0.5, 0.3125, ((1, 8),))
    patches = scatter_about(arg_keys[2], (PATCHES, DV), 1.0, 6.0, ((0, 64), (1, 8)))
    vit_up = scatter_about(arg_keys[3], (DV, FFV), DV ** -0.5, 0.15625, ((1, 8),))
    vit_down = scatter_about(arg_keys[4], (FFV, DV), FFV ** -0.5, 0.078125, ((0, 8),))
    audio_proj = scatter_about(arg_keys[5], (DA, DL), DA ** -0.5, 0.15625, ((0, 64), (1, 8)))
    merger = scatter_about(arg_keys[6], (4 * DV, DL), (4 * DV) ** -0.5, 0.078125, ((0, 64), (1, 8)))
    text_rows = scatter_about(arg_keys[7], (SEQ_DEV, OWNERS, DL), 1.0, 6.0, ((1, 64), (2, 8)))
    span_order = draw_span_order(jax.random.fold_in(arg_keys[12], 71), 0)
    offsets = draw_offsets(jax.random.fold_in(arg_keys[12], 71), 0)
    audio_count = draw_audio_count(jax.random.fold_in(arg_keys[12], 71), 0)
    video_count = draw_video_count(jax.random.fold_in(arg_keys[12], 71), 0)
    return {"mel_frames": mel_frames, "conv_weight": conv_weight, "patches": patches, "vit_up": vit_up, "vit_down": vit_down, "audio_proj": audio_proj, "merger": merger, "text_rows": text_rows, "span_order": span_order, "offsets": offsets, "audio_count": audio_count, "video_count": video_count}


def reference(mel_frames, conv_weight, patches, vit_up, vit_down, audio_proj, merger, text_rows, span_order, offsets, audio_count, video_count):
    odd_rows = mel_frames[1::2]
    earlier = jnp.concatenate([jnp.zeros((1, mel_frames.shape[1]), mel_frames.dtype), odd_rows[:-1]], axis=0)
    stacked = jnp.concatenate([earlier, mel_frames[0::2], odd_rows], axis=1)
    active = jax.nn.gelu(jnp.dot(stacked, conv_weight, preferred_element_type=jnp.float32), approximate=False)
    pooled = (0.5 * (active[0::2] + active[1::2])).astype(jnp.bfloat16)
    audio_rows = jnp.dot(pooled, audio_proj, preferred_element_type=jnp.float32).astype(jnp.bfloat16)
    groups = patches.reshape(NCH, 4 * VT, DV)

    def encode(patch_group):
        widened = patch_group.astype(jnp.float32)
        average = lax.optimization_barrier(jnp.mean(widened, axis=1, keepdims=True))
        centred = widened - average
        spread = lax.optimization_barrier(jnp.mean(centred * centred, axis=1, keepdims=True))
        normed = (centred * lax.rsqrt(spread + 1e-06)).astype(jnp.bfloat16)
        hidden = jax.nn.gelu(jnp.dot(normed, vit_up, preferred_element_type=jnp.float32), approximate=False).astype(jnp.bfloat16)
        vit_out = (widened + jnp.dot(hidden, vit_down, preferred_element_type=jnp.float32)).astype(jnp.bfloat16)
        merged = vit_out.reshape(VT, 4 * DV)
        return jnp.dot(merged, merger, preferred_element_type=jnp.float32).astype(jnp.bfloat16)
    video_rows = lax.map(encode, groups)
    span_start = jnp.zeros((NCH,), jnp.int32).at[span_order].set(offsets.astype(jnp.int32))
    video_index = jnp.arange(VT, dtype=jnp.int32)[None, :]
    video_place = jnp.where(video_index < video_count[:, None], span_start[:, None] + video_index, SEQ)
    audio_index = jnp.arange(AT, dtype=jnp.int32)[None, :]
    audio_place = jnp.where(audio_index < audio_count[:, None], span_start[:, None] + video_count[:, None] + audio_index, SEQ)
    sequence_rows = text_rows.reshape(SEQ, DL)
    sequence_rows = sequence_rows.at[video_place.reshape(-1).astype(jnp.int32)].set(video_rows.reshape(NCH * VT, DL), mode='drop')
    sequence_rows = sequence_rows.at[audio_place.reshape(-1).astype(jnp.int32)].set(audio_rows, mode='drop')
    return sequence_rows.reshape(SEQ_DEV, OWNERS, DL)
```

```python
import jax
import jax.numpy as jnp
from jax import lax
from jax.sharding import Mesh, PartitionSpec as P

AT = 50
VT = 64
BF = jnp.bfloat16
F32 = jnp.float32
TM = ("x", "z")
MP = ("y", "core")


def span_starts(span_order, offsets):
    listed = jnp.arange(span_order.shape[0], dtype=jnp.int32)
    matches = (span_order[:, None] == listed[None, :]).astype(jnp.int32)
    return jnp.sum(matches * offsets[:, None], axis=0)


def ring(value, axis, step):
    count = lax.axis_size(axis)
    return lax.ppermute(value, axis, [(i, (i + step) % count) for i in range(count)])


def gather_x(value):
    return [value] + [ring(value, "x", k) for k in (1, 3, 2)]


def gelu(value):
    return jax.nn.gelu(value, approximate=False)


def dot(a, b):
    return jnp.dot(a, b, preferred_element_type=F32)


def local(
    mel_frames,
    conv_weight,
    patches,
    vit_up,
    vit_down,
    audio_proj,
    merger,
    text_rows,
    span_order,
    offsets,
    audio_count,
    video_count,
):
    owners = lax.axis_size("x") * lax.axis_size("z")
    nx, nz, ny = (lax.axis_size(a) for a in ("x", "z", "y"))
    position = lax.axis_index(TM)
    my_x, my_y, my_core = (lax.axis_index(a) for a in ("x", "y", "core"))
    spans = mel_frames.shape[0] // (4 * AT)
    tokens = spans * owners
    half = tokens // 2
    columns = merger.shape[1]

    with jax.named_scope("weights_x"):
        own = jnp.concatenate([merger, audio_proj], axis=0)
        parts = gather_x(own)
        rows_m, rows_a = merger.shape[0], audio_proj.shape[0]
        block = jnp.concatenate([p[:rows_m] for p in parts] + [p[rows_m:] for p in parts], axis=0)
    with jax.named_scope("weights_z"):
        weights = lax.all_gather(block, "z", axis=0, tiled=False)

    with jax.named_scope("route"):
        starts = span_starts(span_order, offsets)
        first_span = position * spans
        local_start = lax.dynamic_slice_in_dim(starts, first_span, spans)[None, :]
        local_video = lax.dynamic_slice_in_dim(video_count, first_span, spans)[None, :]
        owner_ids = jnp.arange(owners, dtype=jnp.int32)[:, None]
        span_ids = jnp.arange(spans, dtype=jnp.int32)[None, :]
        video_index = jnp.mod(owner_ids - local_start, owners) + span_ids * VT
        token_rows = patches.reshape(spans * VT, -1)
        video_send = token_rows[video_index.reshape(-1)].reshape(owners, spans, -1)
        video_in = lax.all_to_all(video_send, TM, 0, 0, tiled=True).reshape(tokens, -1)

    with jax.named_scope("audio_conv"):
        last = owners - 1
        rim = lax.ppermute(mel_frames[-1:], TM, [(i, i + 1) for i in range(last)])
        f0, f1, f2, f3 = (mel_frames[k::4] for k in range(4))
        before = jnp.concatenate([rim, f3[:-1]], axis=0)
        even = dot(jnp.concatenate([before, f0, f1], axis=1), conv_weight)
        odd = dot(jnp.concatenate([f1, f2, f3], axis=1), conv_weight)
        pooled = (0.5 * (gelu(even) + gelu(odd))).astype(BF)
        audio_index = jnp.minimum(jnp.mod(owner_ids - local_start - local_video, owners), AT - 1)
        audio_index = (audio_index + span_ids * AT).reshape(-1)
        audio_send = pooled[audio_index].reshape(owners, spans, -1)
        audio_in = lax.all_to_all(audio_send, TM, 0, 0, tiled=True).reshape(tokens, -1)

    with jax.named_scope("core_swap"):
        swap = lambda v: lax.ppermute(v, "core", [(0, 1), (1, 0)])
        up_other, down_other = swap(vit_up), swap(vit_down)

        def pair(value, width):
            mine = lax.dynamic_slice_in_dim(value, my_core * half, half)
            theirs = swap(lax.dynamic_slice_in_dim(value, (1 - my_core) * half, half))
            mine, theirs = (v.reshape(half, -1, width) for v in (mine, theirs))
            first = jnp.where(my_core == 0, mine, theirs)
            second = jnp.where(my_core == 0, theirs, mine)
            return jnp.concatenate([first, second], axis=2).reshape(half, -1)

        width = patches.shape[1]
        video_pair = pair(video_in, width)
        audio_pair = pair(audio_in, width)

    with jax.named_scope("gather_y"):
        video_y = lax.all_gather(video_pair, "y", axis=0, tiled=False)
        video_y = video_y.reshape(ny, half, 4, 2 * width)
        rows = jnp.transpose(video_y, (2, 1, 0, 3)).reshape(4 * half, ny * 2 * width)

    with jax.named_scope("vision"):
        widened = rows.astype(F32)
        average = jnp.mean(widened, axis=1, keepdims=True)
        centred = widened - average
        spread = jnp.mean(centred * centred, axis=1, keepdims=True)
        normed = (centred * lax.rsqrt(spread + 1e-06)).astype(BF)
        hidden = gelu(dot(normed, vit_up)).astype(BF)
        hidden_other = gelu(dot(normed, up_other)).astype(BF)
        partial_sum = dot(hidden, vit_down) + dot(hidden_other, down_other)
        partial_sum = partial_sum.astype(BF).reshape(4, half, -1)

    with jax.named_scope("sum_y"):
        full_width = partial_sum.shape[2]
        audio_flat = audio_pair.reshape(-1, full_width)
        audio_rows_n = audio_flat.shape[0]
        pad = -audio_rows_n % 16
        audio_flat = jnp.pad(audio_flat, ((0, pad), (0, 0)))
        audio_all = jnp.broadcast_to(audio_flat, (ny,) + audio_flat.shape)
        outgoing = jnp.concatenate([partial_sum, audio_all], axis=1)
        incoming = lax.all_to_all(outgoing, "y", 0, 0, tiled=True)
        residual = lax.dynamic_index_in_dim(rows.reshape(4, half, -1), my_y, 0, keepdims=False)
        summed = jnp.sum(incoming[:, :half].astype(F32), axis=0)
        vit_out = (residual.astype(F32) + summed).astype(BF)
        audio_y = incoming[:, half : half + audio_rows_n].reshape(ny, half, 2 * width)
        audio_tok = jnp.transpose(audio_y, (1, 0, 2)).reshape(half, -1)

    with jax.named_scope("gather_vit"):
        vit_y = lax.all_gather(vit_out, "y", axis=0, tiled=False)
        both = jnp.concatenate([vit_y, audio_tok[None]], axis=0)
        other = swap(both)
        low = jnp.where(my_core == 0, both, other)
        high = jnp.where(my_core == 0, other, both)
        both = jnp.concatenate([low, high], axis=1)

    with jax.named_scope("project"):
        zm = nx * rows_m
        merge_w = weights[:, :zm].reshape(nz, nx, rows_m, columns)
        audio_w = weights[:, zm:].reshape(nz, nx, rows_a, columns)
        order = jnp.array([0, 1, 3, 2], jnp.int32)
        slot = order[jnp.mod(my_x - jnp.arange(nx), nx)]
        merge_w = jnp.transpose(merge_w[:, slot], (1, 0, 2, 3)).reshape(-1, columns)
        audio_w = jnp.transpose(audio_w[:, slot], (1, 0, 2, 3)).reshape(-1, columns)
        merged = jnp.transpose(both[:4], (1, 0, 2)).reshape(tokens, -1)
        video_rows = dot(merged, merge_w).astype(BF)
        audio_rows = dot(both[4], audio_w).astype(BF)

    with jax.named_scope("place"):
        seq_count = text_rows.shape[0]
        video_where = jnp.mod(position - starts, owners)
        video_place = jnp.where(
            video_where < video_count, (starts + video_where) // owners, seq_count
        )
        audio_where = jnp.mod(position - starts - video_count, owners)
        audio_place = jnp.where(
            audio_where < audio_count, (starts + video_count + audio_where) // owners, seq_count
        )
        slot_rows = jnp.concatenate([video_place, audio_place])
        media = jnp.concatenate([video_rows, audio_rows], axis=0)
        sequence_rows = text_rows[:, 0, :].at[slot_rows].set(media, mode="drop")
    return sequence_rows[:, None, :]


def solution(mesh):
    grid = Mesh(mesh.devices.reshape(4, 16, 4, 2), ("x", "z", "y", "core"))
    placed = (
        P(TM, None),
        P(None, MP),
        P(TM, MP),
        P(None, MP),
        P(MP, None),
        P(TM, MP),
        P(TM, MP),
        P(None, TM, MP),
        P(),
        P(),
        P(),
        P(),
    )
    return jax.shard_map(
        local, mesh=grid, in_specs=placed, out_specs=P(None, TM, MP), check_vma=False
    )
```

```python
import jax
import jax.numpy as jnp
from jax import lax
from jax.experimental import pallas as pl
from jax.experimental.pallas import tpu as pltpu
from jax.sharding import Mesh, PartitionSpec as P

AT = 50
VT = 64
BF = jnp.bfloat16
F32 = jnp.float32
I32 = jnp.int32
TM = ("x", "z")
MP = ("y", "core")
PAD_A = 32
VMEM = pl.BlockSpec(memory_space=pltpu.VMEM)
SMEM = pl.BlockSpec(memory_space=pltpu.SMEM)
ANY = pl.BlockSpec(memory_space=pl.ANY)
ROOT_HALF = 0.7071067811865476


def span_starts(span_order, offsets):
    listed = jnp.arange(span_order.shape[0], dtype=I32)
    matches = (span_order[:, None] == listed[None, :]).astype(I32)
    return jnp.sum(matches * offsets[:, None], axis=0)


def ring(value, axis, step):
    count = lax.axis_size(axis)
    return lax.ppermute(value, axis, [(i, (i + step) % count) for i in range(count)])


def swap(value):
    return lax.ppermute(value, "core", [(0, 1), (1, 0)])


def gelu(value):
    return 0.5 * value * (1.0 + lax.erf(value * ROOT_HALF))


def dot(a, b):
    return jnp.dot(a, b, preferred_element_type=F32)


def dot_nt(a, b):
    return lax.dot_general(a, b, (((1,), (1,)), ((), ())), preferred_element_type=F32)


def iota(shape, axis):
    return lax.broadcasted_iota(I32, shape, axis)


def params(mib=48):
    return pltpu.CompilerParams(vmem_limit_bytes=mib * 1024 * 1024)


def one_hot(condition):
    return jnp.where(condition, 1.0, 0.0).astype(BF)


def prep_kernel(first_ref, audio_ref, patch_ref, mel_ref, rim_ref, conv_ref, out_ref):
    rows, width = out_ref.shape
    spans, count = 3, patch_ref.shape[1]
    block = patch_ref.shape[0]
    patch = patch_ref[...]
    row = iota((rows, 1), 0)
    owner, kind = row >> 2, row & 3
    start = jnp.where(kind == 0, first_ref[0], jnp.where(kind == 1, first_ref[1], first_ref[2]))
    token = (kind << 6) + ((owner - start) & (VT - 1))
    target = jnp.where(kind < spans, token * 4, -8)
    column = iota((rows, count), 1)
    source = iota((block, width), 0)
    place = iota((block, width), 1)
    total = jnp.zeros((rows, width), F32)
    for s in range(4):
        picked = dot_nt(one_hot(column == target + s), patch).astype(BF)
        total += dot(picked, one_hot(place == source + s * block))

    frames = mel_ref.shape[0]
    f0, f1, f2, f3 = (mel_ref[:, k * 128 : (k + 1) * 128] for k in range(4))
    behind = one_hot(iota((frames, frames), 1) == iota((frames, frames), 0) - 1)
    first_row = iota((frames, 1), 0) == 0
    before = dot(behind, f3) + jnp.where(first_row, rim_ref[...].astype(F32), 0.0)
    before = before.astype(BF)
    c0, c1, c2 = (conv_ref[k * 128 : (k + 1) * 128, :] for k in range(3))
    even = dot(before, c0) + dot(f0, c1) + dot(f1, c2)
    odd = dot(f1, c0) + dot(f2, c1) + dot(f3, c2)
    pooled = (0.5 * (gelu(even) + gelu(odd))).astype(BF)
    column = iota((rows, frames), 1)
    for i in range(spans):
        index = jnp.minimum((owner - audio_ref[i]) & (VT - 1), AT - 1) + i * AT
        index = jnp.where(kind == spans, index, -8)
        picked = dot(one_hot(column == index), pooled).astype(BF)
        total += dot(picked, one_hot(place == source + i * block))
    out_ref[...] = total.astype(BF)


def vision_kernel(
    index_ref, video_ref, up0, down0, up1, down1, send_ref, rest_ref, xs, wu, wd, sems
):
    copies = []
    for i, (u, d) in enumerate(((up0, down0), (up1, down1))):
        copies.append(pltpu.make_async_copy(u, wu.at[i], sems.at[2 * i]))
        copies.append(pltpu.make_async_copy(d, wd.at[i], sems.at[2 * i + 1]))
    for copy in copies:
        copy.start()
    my_y = index_ref[0]
    ny, cores, half, width = video_ref.shape
    block = width // 4
    for y in range(ny):
        for c in range(cores):
            for s in range(4):
                a, b = (y * cores + c) * block, s * block
                xs[s * half : (s + 1) * half, a : a + block] = video_ref[y, c, :, b : b + block]
    wide = xs[...].astype(F32)
    centred = wide - jnp.mean(wide, axis=1, keepdims=True)
    spread = jnp.mean(centred * centred, axis=1, keepdims=True)
    normed = (centred * lax.rsqrt(spread + 1e-06)).astype(BF)
    total = None
    for i in range(2):
        copies[2 * i].wait()
        hidden = gelu(dot(normed, wu[i])).astype(BF)
        copies[2 * i + 1].wait()
        term = dot(hidden, wd[i])
        total = term if total is None else total + term
    total = total.astype(BF)
    for s in range(4):
        send_ref[s] = total[s * half : (s + 1) * half]
    begin = pl.multiple_of(my_y * half, half)
    rest_ref[...] = xs[pl.ds(begin, half), :]


def audio_kernel(index_ref, a_ref, b_ref, c_ref, d_ref, out_ref):
    my_y = index_ref[0]
    owners = a_ref.shape[0] // 2
    block = a_ref.shape[1] // 3
    source, place = iota((block, 256), 0), iota((block, 256), 1)
    group = place // PAD_A
    lane = place - group * PAD_A
    spread = one_hot((lane < 20) & (source == group * 20 + lane))
    for ref, far in ((a_ref, 0), (b_ref, 1), (c_ref, 3), (d_ref, 2)):
        y = (my_y - far) & 3
        for k in range(3):
            piece = dot(ref[:, k * block : (k + 1) * block], spread).astype(BF)
            for c in range(2):
                out_ref[y, k * owners : (k + 1) * owners, c * 256 : (c + 1) * 256] = piece[
                    c * owners : (c + 1) * owners
                ]


def tail_kernel(
    own_ref, other_ref, audio_ref, weight_ref, place_ref, text_ref, out_ref, video, audio
):
    step = pl.program_id(0)

    @pl.when(step == 0)
    def _():
        video[...] = jnp.zeros_like(video)
        audio[...] = jnp.zeros_like(audio)

    nz, _, rows, columns = weight_ref.shape
    rows_m = rows - PAD_A
    merge_w = weight_ref[:, 0, :rows_m, :].reshape(nz * rows_m, columns)
    audio_w = weight_ref[:, 0, rows_m:, :].reshape(nz * PAD_A, columns)
    both = jnp.concatenate([own_ref[0], other_ref[0]], axis=0)
    video[...] += dot(both, merge_w)
    audio[...] += dot(audio_ref[0], audio_w)

    @pl.when(step == 3)
    def _():
        media = jnp.concatenate([video[...], audio[...]], axis=0).astype(BF)
        count, length = media.shape[0], out_ref.shape[1]
        marks = one_hot(place_ref[...] == iota((length, count), 0))
        placed = lax.dot_general(
            media, marks, (((0,), (1,)), ((), ())), preferred_element_type=F32
        )
        taken = dot_nt(jnp.ones((8, count), BF), marks)[0:1, :]
        out_ref[...] = jnp.where(taken > 0.5, placed, text_ref[...].astype(F32)).astype(BF)


def local(
    mel_frames,
    conv_weight,
    patches,
    vit_up,
    vit_down,
    audio_proj,
    merger,
    text_rows,
    span_order,
    offsets,
    audio_count,
    video_count,
):
    nx, nz, ny = (lax.axis_size(a) for a in ("x", "z", "y"))
    owners = nx * nz
    position = lax.axis_index(TM)
    my_y, my_core = lax.axis_index("y"), lax.axis_index("core")
    spans = mel_frames.shape[0] // (4 * AT)
    tokens = spans * owners
    half, near = tokens // 2, owners // 2
    columns, rows_m, rows_a = merger.shape[1], merger.shape[0], audio_proj.shape[0]
    rows_w = rows_m + PAD_A
    width = 4 * patches.shape[1]
    full = vit_down.shape[1]

    rim = lax.ppermute(mel_frames[-1:], TM, [(i, i + 1) for i in range(owners - 1)])

    own = jnp.concatenate([merger, audio_proj, jnp.zeros((PAD_A - rows_a, columns), BF)], axis=0)
    block = lax.all_gather(own, "x", axis=0, tiled=False)
    weights = lax.all_gather(block, "z", axis=0, tiled=False)

    starts = span_starts(span_order, offsets)
    local_start = lax.dynamic_slice_in_dim(starts, position * spans, spans)
    local_video = lax.dynamic_slice_in_dim(video_count, position * spans, spans)
    outgoing = pl.pallas_call(
        prep_kernel,
        name="prep",
        out_shape=jax.ShapeDtypeStruct((owners * (spans + 1), width), BF),
        in_specs=[SMEM, SMEM, VMEM, VMEM, VMEM, VMEM],
        out_specs=VMEM,
        compiler_params=params(),
    )(
        local_start,
        local_start + local_video,
        patches.T,
        mel_frames.reshape(spans * AT, -1),
        rim,
        conv_weight,
    )
    arrived = lax.all_to_all(
        outgoing.reshape(owners, spans + 1, width), TM, 0, 0, tiled=True
    )

    up_other, down_other = swap(vit_up), swap(vit_down)
    cores = lax.all_gather(arrived, "core", axis=0, tiled=False)
    pair = lax.dynamic_slice_in_dim(cores, my_core * near, near, axis=1)[:, :, :spans]
    video_pair = jnp.transpose(pair, (0, 2, 1, 3)).reshape(2, half, width)
    video_y = lax.all_gather(video_pair, "y", axis=0, tiled=False)

    where_am_i = jnp.stack([my_y]).astype(I32)
    flops = 2 * 4 * half * full * 4 * vit_up.shape[1]
    partial_sum, residual = pl.pallas_call(
        vision_kernel,
        name="vision",
        out_shape=(
            jax.ShapeDtypeStruct((4, half, full), BF),
            jax.ShapeDtypeStruct((half, full), BF),
        ),
        in_specs=[SMEM, VMEM, ANY, ANY, ANY, ANY],
        out_specs=(VMEM, VMEM),
        scratch_shapes=[
            pltpu.VMEM((4 * half, full), BF),
            pltpu.VMEM((2,) + vit_up.shape, BF),
            pltpu.VMEM((2,) + vit_down.shape, BF),
            pltpu.SemaphoreType.DMA((4,)),
        ],
        compiler_params=params(),
        cost_estimate=pl.CostEstimate(flops=flops, bytes_accessed=9000000, transcendentals=500000),
    )(where_am_i, video_y, vit_up, vit_down, up_other, down_other)

    audio_own = cores[:, :, spans, : spans * patches.shape[1]].reshape(2 * owners, -1)
    audio_own, partial_sum = lax.optimization_barrier((audio_own, partial_sum))
    incoming = lax.all_to_all(partial_sum, "y", 0, 0, tiled=True)
    audio_y = [audio_own] + [ring(audio_own, "y", k) for k in (1, 3, 2)]
    audio_tokens = pl.pallas_call(
        audio_kernel,
        name="audio_spread",
        out_shape=jax.ShapeDtypeStruct((ny, tokens, nz * PAD_A), BF),
        in_specs=[SMEM] + [VMEM] * 4,
        out_specs=VMEM,
        compiler_params=params(),
    )(where_am_i, *audio_y)
    summed = jnp.sum(incoming.astype(F32), axis=0)
    vit_out = (residual.astype(F32) + summed).astype(BF)
    vit_out, audio_tokens = lax.optimization_barrier((vit_out, audio_tokens))
    vit_mine = lax.all_gather(vit_out, "y", axis=0, tiled=False)
    vit_theirs = swap(vit_mine)

    seq_count = text_rows.shape[0]
    video_where = jnp.mod(position - starts, owners)
    video_place = jnp.where(video_where < video_count, (starts + video_where) // owners, seq_count)
    audio_where = jnp.mod(position - starts - video_count, owners)
    audio_place = jnp.where(
        audio_where < audio_count, (starts + video_count + audio_where) // owners, seq_count
    )

    video_place = video_place.reshape(2, near, spans)
    video_place = jnp.where(my_core == 0, video_place, video_place[::-1])
    video_place = jnp.transpose(video_place, (0, 2, 1)).reshape(-1)
    audio_place = audio_place.reshape(owners, spans).T.reshape(-1)
    places = jnp.concatenate([video_place, audio_place])
    result = pl.pallas_call(
        tail_kernel,
        name="project_place",
        out_shape=jax.ShapeDtypeStruct((columns, seq_count), BF),
        grid_spec=pl.GridSpec(
            grid=(4,),
            in_specs=[
                pl.BlockSpec((1, half, full), lambda s: (s, 0, 0)),
                pl.BlockSpec((1, half, full), lambda s: (s, 0, 0)),
                pl.BlockSpec((1, tokens, nz * PAD_A), lambda s: (s, 0, 0)),
                pl.BlockSpec((nz, 1, rows_w, columns), lambda s: (0, s, 0, 0)),
                pl.BlockSpec((1, 2 * tokens), lambda s: (0, 0)),
                pl.BlockSpec((columns, seq_count), lambda s: (0, 0)),
            ],
            out_specs=pl.BlockSpec((columns, seq_count), lambda s: (0, 0)),
            scratch_shapes=[pltpu.VMEM((tokens, columns), F32), pltpu.VMEM((tokens, columns), F32)],
        ),
        compiler_params=params(),
        cost_estimate=pl.CostEstimate(flops=1100000000, bytes_accessed=9000000, transcendentals=0),
    )(
        vit_mine,
        vit_theirs,
        audio_tokens,
        weights.reshape(nz, nx, rows_w, columns),
        places.reshape(1, -1),
        text_rows[:, 0, :].T,
    )
    return result.T[:, None, :]


def solution(mesh):
    grid = Mesh(mesh.devices.reshape(4, 16, 4, 2), ("x", "z", "y", "core"))
    placed = (
        P(TM, None),
        P(None, MP),
        P(TM, MP),
        P(None, MP),
        P(MP, None),
        P(TM, MP),
        P(TM, MP),
        P(None, TM, MP),
        P(),
        P(),
        P(),
        P(),
    )
    return jax.shard_map(
        local, mesh=grid, in_specs=placed, out_specs=P(None, TM, MP), check_vma=False
    )
```

```python
import jax
import jax.numpy as jnp
from jax import lax
from jax.experimental import pallas as pl
from jax.experimental.pallas import tpu as pltpu
from jax.sharding import Mesh, PartitionSpec as P

AT = 50
VT = 64
BF = jnp.bfloat16
F32 = jnp.float32
I32 = jnp.int32
TM = ("x", "z")
MP = ("y", "core")
PAD_A = 32
VMEM = pl.BlockSpec(memory_space=pltpu.VMEM)
SMEM = pl.BlockSpec(memory_space=pltpu.SMEM)
ANY = pl.BlockSpec(memory_space=pl.ANY)
ROOT_HALF = 0.7071067811865476


def span_starts(span_order, offsets):
    listed = jnp.arange(span_order.shape[0], dtype=I32)
    matches = (span_order[:, None] == listed[None, :]).astype(I32)
    return jnp.sum(matches * offsets[:, None], axis=0)


def ring(value, axis, step):
    count = lax.axis_size(axis)
    return lax.ppermute(value, axis, [(i, (i + step) % count) for i in range(count)])


def swap(value):
    return lax.ppermute(value, "core", [(0, 1), (1, 0)])


def gelu(value):
    return 0.5 * value * (1.0 + lax.erf(value * ROOT_HALF))


def dot(a, b):
    return jnp.dot(a, b, preferred_element_type=F32)


def dot_nt(a, b):
    return lax.dot_general(a, b, (((1,), (1,)), ((), ())), preferred_element_type=F32)


def iota(shape, axis):
    return lax.broadcasted_iota(I32, shape, axis)


def params(mib=48):
    return pltpu.CompilerParams(vmem_limit_bytes=mib * 1024 * 1024)


def one_hot(condition):
    return jnp.where(condition, 1.0, 0.0).astype(BF)


def prep_kernel(
    order_ref, offset_ref, video_ref, patch_ref, mel_ref, rim_ref, conv_ref, out_ref
):
    rows, width = out_ref.shape
    spans, count = 3, patch_ref.shape[1]
    block = patch_ref.shape[0]
    nx, nz = lax.axis_size("x"), lax.axis_size("z")
    videos = nx * spans
    position = lax.axis_index("x") * lax.axis_size("z") + lax.axis_index("z")
    listed = iota(order_ref.shape, 1)

    def pick(condition, values):
        return jnp.sum(jnp.where(condition, values, 0), axis=1, keepdims=True)

    first = [pick(order_ref[...] == position * spans + k, offset_ref[...]) for k in range(spans)]
    kept = [pick(listed == position * spans + k, video_ref[...]) for k in range(spans)]
    patch = patch_ref[...]
    row = iota((rows, 1), 0)
    far, slot = row >> 4, row & 15
    to_x = sum((slot >= spans * i).astype(I32) for i in range(1, nx))
    is_video = slot < videos
    kind = jnp.where(is_video, slot - spans * to_x, slot - videos)

    def of_kind(values):
        return jnp.where(kind == 0, values[0], jnp.where(kind == 1, values[1], values[2]))

    start = of_kind(first)
    token = (kind << 6) + ((to_x * nz + far - start) & (VT - 1))
    target = jnp.where(is_video, token * 4, -8)
    column = iota((rows, count), 1)
    source = iota((block, width), 0)
    place = iota((block, width), 1)
    total = jnp.zeros((rows, width), F32)
    for s in range(4):
        picked = dot_nt(one_hot(column == target + s), patch).astype(BF)
        total += dot(picked, one_hot(place == source + s * block))

    total_frames = mel_ref.shape[0]
    frames = total_frames // 4
    frame, at = iota((frames, total_frames), 1), 4 * iota((frames, total_frames), 0)
    mel = mel_ref[...]
    before, f0, f1, f2, f3 = (dot(one_hot(frame == at + k), mel).astype(BF) for k in range(-1, 4))
    first_row = iota((frames, 1), 0) == 0
    before = jnp.where(first_row, rim_ref[...].astype(F32), before.astype(F32)).astype(BF)
    c0, c1, c2 = (conv_ref[k * 128 : (k + 1) * 128, :] for k in range(3))
    even = dot(before, c0) + dot(f0, c1) + dot(f1, c2)
    odd = dot(f1, c0) + dot(f2, c1) + dot(f3, c2)
    pooled = (0.5 * (gelu(even) + gelu(odd))).astype(BF)
    column = iota((rows, frames), 1)
    start = start + of_kind(kept)
    for i in range(nx):
        index = jnp.minimum((i * nz + far - start) & (VT - 1), AT - 1) + kind * AT
        index = jnp.where(is_video | (kind >= spans), -8, index)
        picked = dot(one_hot(column == index), pooled).astype(BF)
        total += dot(picked, one_hot(place == source + i * block))
    out_ref[...] = total.astype(BF)


def vision_kernel(
    video_ref, audio_ref, up0, down0, up1, down1, send_ref, xs, wu, wd, sems
):
    copies = []
    for i, (u, d) in enumerate(((up0, down0), (up1, down1))):
        copies.append(pltpu.make_async_copy(u, wu.at[i], sems.at[2 * i]))
        copies.append(pltpu.make_async_copy(d, wd.at[i], sems.at[2 * i + 1]))
    for copy in copies:
        copy.start()
    ny, cores, half, width = video_ref.shape
    block = width // 4
    for y in range(ny):
        for c in range(cores):
            for s in range(4):
                a, b = (y * cores + c) * block, s * block
                xs[s * half : (s + 1) * half, a : a + block] = video_ref[y, c, :, b : b + block]
    wide = xs[...].astype(F32)
    centred = wide - jnp.mean(wide, axis=1, keepdims=True)
    spread = jnp.mean(centred * centred, axis=1, keepdims=True)
    normed = (centred * lax.rsqrt(spread + 1e-06)).astype(BF)
    total = None
    for i in range(2):
        copies[2 * i].wait()
        hidden = gelu(dot(normed, wu[i])).astype(BF)
        copies[2 * i + 1].wait()
        term = dot(hidden, wd[i])
        total = term if total is None else total + term
    total += wide * (1.0 / ny)
    parts = send_ref.shape[0] // 4
    some = half // parts
    send_ref[...] = jnp.zeros_like(send_ref)
    for s in range(4):
        for x in range(parts):
            a = s * half + x * some
            send_ref[x * ny + s, :some] = total[a : a + some].astype(BF)
            for c in range(cores):
                for k in range(3):
                    a, b = (c * 3 + k) * block, x * block
                    send_ref[x * ny + s, some:, a : a + block] = audio_ref[c, k, :, b : b + block]


def audio_kernel(in_ref, out_ref):
    ny, tokens, _ = out_ref.shape
    block, parts = in_ref.shape[2] // 8, in_ref.shape[0] // ny
    owners = tokens // 3
    near = owners // parts
    some = in_ref.shape[1] - near
    source, place = iota((block, 256), 0), iota((block, 256), 1)
    group = place // PAD_A
    lane = place - group * PAD_A
    spread = one_hot((lane < 20) & (source == group * 20 + lane))
    for y in range(ny):
        for c in range(2):
            for k in range(3):
                a = (c * 3 + k) * block
                rows = [in_ref[x * ny + y, some:, a : a + block] for x in range(parts)]
                piece = dot(jnp.concatenate(rows, axis=0), spread).astype(BF)
                out_ref[y, k * owners : (k + 1) * owners, c * 256 : (c + 1) * 256] = piece


def tail_kernel(
    own_ref, other_ref, audio_ref, weight_ref, place_ref, text_ref, out_ref, video, audio, spread
):
    step = pl.program_id(0)

    @pl.when(step == 0)
    def _():
        video[...] = jnp.zeros_like(video)
        audio[...] = jnp.zeros_like(audio)
        spread[...] = jnp.zeros_like(spread)

    nz, _, rows, columns = weight_ref.shape
    rows_a = rows // 5
    rows_m = rows - rows_a
    merge_w = weight_ref[:, 0, :rows_m, :].reshape(nz * rows_m, columns)
    for z in range(nz):
        spread[z * PAD_A : z * PAD_A + rows_a, :] = weight_ref[z, 0, rows_m:, :]
    both = jnp.concatenate([own_ref[0], other_ref[0]], axis=0)
    video[...] += dot(both, merge_w)
    audio[...] += dot(audio_ref[0], spread[...])

    @pl.when(step == 3)
    def _():
        media = jnp.concatenate([video[...], audio[...]], axis=0).astype(BF)
        count, length = media.shape[0], out_ref.shape[1]
        marks = one_hot(place_ref[...] == iota((length, count), 0))
        placed = lax.dot_general(
            media, marks, (((0,), (1,)), ((), ())), preferred_element_type=F32
        )
        taken = dot_nt(jnp.ones((8, count), BF), marks)[0:1, :]
        out_ref[...] = jnp.where(taken > 0.5, placed, text_ref[...].astype(F32)).astype(BF)


def local(
    mel_frames,
    conv_weight,
    patches,
    vit_up,
    vit_down,
    audio_proj,
    merger,
    text_rows,
    span_order,
    offsets,
    audio_count,
    video_count,
):
    nx, nz, ny = (lax.axis_size(a) for a in ("x", "z", "y"))
    owners = nx * nz
    position = lax.axis_index(TM)
    my_core = lax.axis_index("core")
    spans = mel_frames.shape[0] // (4 * AT)
    tokens = spans * owners
    half = tokens // 2
    columns, rows_m, rows_a = merger.shape[1], merger.shape[0], audio_proj.shape[0]
    rows_w = rows_m + rows_a
    width = 4 * patches.shape[1]
    full = vit_down.shape[1]

    rim = lax.ppermute(mel_frames[-1:], TM, [(i, i + 1) for i in range(owners - 1)])

    own = jnp.concatenate([merger, audio_proj], axis=0)
    rim, own = lax.optimization_barrier((rim, own))
    everywhere = jnp.broadcast_to(own[None], (nx,) + own.shape)
    block = lax.all_to_all(everywhere, "x", 0, 0, tiled=True)

    starts = span_starts(span_order, offsets)
    outgoing = pl.pallas_call(
        prep_kernel,
        name="prep",
        out_shape=jax.ShapeDtypeStruct((nz * 16, width), BF),
        in_specs=[VMEM] * 7,
        out_specs=VMEM,
        compiler_params=params(),
        cost_estimate=pl.CostEstimate(
            flops=2000000000, bytes_accessed=8000000, transcendentals=500000
        ),
    )(
        span_order.reshape(1, -1),
        offsets.reshape(1, -1),
        video_count.reshape(1, -1),
        patches.T,
        mel_frames,
        rim,
        conv_weight,
    )
    block, outgoing = lax.optimization_barrier((block, outgoing))
    weights = lax.all_gather(block, "z", axis=0, tiled=False)
    arrived = lax.all_to_all(outgoing.reshape(nz, 16, width), "z", 0, 0, tiled=True)

    up_other, down_other = swap(vit_up), swap(vit_down)
    cores = lax.all_gather(arrived, "core", axis=0, tiled=False)
    videos, half_z = nx * spans, nz // 2
    pair = lax.dynamic_slice_in_dim(cores, my_core * half_z, half_z, axis=1)[:, :, :videos]
    pair = pair.reshape(2, half_z, nx, spans, width)
    video_pair = jnp.transpose(pair, (0, 2, 1, 3, 4)).reshape(2, half, width)
    video_y = lax.all_gather(video_pair, "y", axis=0, tiled=False)
    audio_own = jnp.transpose(cores[:, :, videos : videos + spans], (0, 2, 1, 3))

    some = half // nx
    rows_sent = some + nz
    flops = 2 * 4 * half * full * 4 * vit_up.shape[1]
    partial_sum = pl.pallas_call(
        vision_kernel,
        name="vision",
        out_shape=jax.ShapeDtypeStruct((nx * ny, rows_sent, full), BF),
        in_specs=[VMEM, VMEM, ANY, ANY, ANY, ANY],
        out_specs=VMEM,
        scratch_shapes=[
            pltpu.VMEM((4 * half, full), BF),
            pltpu.VMEM((2,) + vit_up.shape, BF),
            pltpu.VMEM((2,) + vit_down.shape, BF),
            pltpu.SemaphoreType.DMA((4,)),
        ],
        compiler_params=params(),
        cost_estimate=pl.CostEstimate(flops=flops, bytes_accessed=9000000, transcendentals=500000),
    )(video_y, audio_own, vit_up, vit_down, up_other, down_other)

    incoming = lax.all_to_all(partial_sum, ("x", "y"), 0, 0, tiled=True)
    audio_tokens = pl.pallas_call(
        audio_kernel,
        name="audio_spread",
        out_shape=jax.ShapeDtypeStruct((ny, tokens, nz * PAD_A), BF),
        in_specs=[VMEM],
        out_specs=VMEM,
        compiler_params=params(),
    )(incoming)
    summed = jnp.sum(incoming.reshape(nx, ny, rows_sent, full)[:, :, :some].astype(F32), axis=1)
    vit_out = summed.astype(BF).reshape(half, full)
    vit_mine = lax.all_gather(vit_out, "y", axis=0, tiled=False)
    vit_theirs = swap(vit_mine)

    seq_count = text_rows.shape[0]
    video_where = jnp.mod(position - starts, owners)
    video_place = jnp.where(video_where < video_count, (starts + video_where) // owners, seq_count)
    audio_where = jnp.mod(position - starts - video_count, owners)
    audio_place = jnp.where(
        audio_where < audio_count, (starts + video_count + audio_where) // owners, seq_count
    )

    video_place = video_place.reshape(nx, 2, half_z, spans)
    video_place = jnp.where(my_core == 0, video_place, video_place[:, ::-1])
    video_place = jnp.transpose(video_place, (1, 0, 2, 3)).reshape(-1)
    audio_place = audio_place.reshape(owners, spans).T.reshape(-1)
    places = jnp.concatenate([video_place, audio_place])
    result = pl.pallas_call(
        tail_kernel,
        name="project_place",
        out_shape=jax.ShapeDtypeStruct((columns, seq_count), BF),
        grid_spec=pl.GridSpec(
            grid=(4,),
            in_specs=[
                pl.BlockSpec((1, half, full), lambda s: (s, 0, 0)),
                pl.BlockSpec((1, half, full), lambda s: (s, 0, 0)),
                pl.BlockSpec((1, tokens, nz * PAD_A), lambda s: (s, 0, 0)),
                pl.BlockSpec((nz, 1, rows_w, columns), lambda s: (0, s, 0, 0)),
                pl.BlockSpec((1, 2 * tokens), lambda s: (0, 0)),
                pl.BlockSpec((columns, seq_count), lambda s: (0, 0)),
            ],
            out_specs=pl.BlockSpec((columns, seq_count), lambda s: (0, 0)),
            scratch_shapes=[
                pltpu.VMEM((tokens, columns), F32),
                pltpu.VMEM((tokens, columns), F32),
                pltpu.VMEM((nz * PAD_A, columns), BF),
            ],
        ),
        compiler_params=params(),
        cost_estimate=pl.CostEstimate(flops=1100000000, bytes_accessed=9000000, transcendentals=0),
    )(
        vit_mine,
        vit_theirs,
        audio_tokens,
        weights.reshape(nz, nx, rows_w, columns),
        places.reshape(1, -1),
        text_rows[:, 0, :].T,
    )
    return result.T[:, None, :]


def solution(mesh):
    grid = Mesh(mesh.devices.reshape(4, 16, 4, 2), ("x", "z", "y", "core"))
    placed = (
        P(TM, None),
        P(None, MP),
        P(TM, MP),
        P(None, MP),
        P(MP, None),
        P(TM, MP),
        P(TM, MP),
        P(None, TM, MP),
        P(),
        P(),
        P(),
        P(),
    )
    return jax.shard_map(
        local, mesh=grid, in_specs=placed, out_specs=P(None, TM, MP), check_vma=False
    )
```

```python
import jax
import jax.numpy as jnp
from jax import lax
from jax.experimental import pallas as pl
from jax.experimental.pallas import tpu as pltpu
from jax.sharding import Mesh, PartitionSpec as P

AT = 50
VT = 64
BF = jnp.bfloat16
F32 = jnp.float32
I32 = jnp.int32
TM = ("x", "z")
MP = ("y", "core")
PAD_A = 32
VMEM = pl.BlockSpec(memory_space=pltpu.VMEM)
SMEM = pl.BlockSpec(memory_space=pltpu.SMEM)
ANY = pl.BlockSpec(memory_space=pl.ANY)
ROOT_HALF = 0.7071067811865476


def span_starts(span_order, offsets):
    listed = jnp.arange(span_order.shape[0], dtype=I32)
    matches = (span_order[:, None] == listed[None, :]).astype(I32)
    return jnp.sum(matches * offsets[:, None], axis=0)


def ring(value, axis, step):
    count = lax.axis_size(axis)
    return lax.ppermute(value, axis, [(i, (i + step) % count) for i in range(count)])


def swap(value):
    return lax.ppermute(value, "core", [(0, 1), (1, 0)])


def gelu(value):
    return 0.5 * value * (1.0 + lax.erf(value * ROOT_HALF))


def dot(a, b):
    return jnp.dot(a, b, preferred_element_type=F32)


def dot_nt(a, b):
    return lax.dot_general(a, b, (((1,), (1,)), ((), ())), preferred_element_type=F32)


def iota(shape, axis):
    return lax.broadcasted_iota(I32, shape, axis)


def params(mib):
    return pltpu.CompilerParams(vmem_limit_bytes=mib * 1024 * 1024)


def whole(shape):
    return pl.BlockSpec(shape, lambda *i: (0,) * len(shape))


def one_hot(condition):
    return jnp.where(condition, 1.0, 0.0).astype(BF)


def prep_kernel(
    order_ref, offset_ref, video_ref, patch_ref, mel_ref, rim_ref, conv_ref, out_ref, wide_mel, shifted
):
    rows, width = out_ref.shape
    spans, count = 3, patch_ref.shape[1]
    block = patch_ref.shape[0]
    nx, nz = lax.axis_size("x"), lax.axis_size("z")
    videos = nx * spans
    position = lax.axis_index("x") * lax.axis_size("z") + lax.axis_index("z")
    listed = iota(order_ref.shape, 1)

    def pick(condition, values):
        return jnp.sum(jnp.where(condition, values, 0), axis=1, keepdims=True)

    first = [pick(order_ref[...] == position * spans + k, offset_ref[...]) for k in range(spans)]
    kept = [pick(listed == position * spans + k, video_ref[...]) for k in range(spans)]
    patch = patch_ref[...]
    row = iota((rows, 1), 0)
    far, slot = row >> 4, row & 15
    to_x = sum((slot >= spans * i).astype(I32) for i in range(1, nx))
    is_video = slot < videos
    kind = jnp.where(is_video, slot - spans * to_x, slot - videos)

    def of_kind(values):
        return jnp.where(kind == 0, values[0], jnp.where(kind == 1, values[1], values[2]))

    start = of_kind(first)
    token = (kind << 6) + ((to_x * nz + far - start) & (VT - 1))
    target = jnp.where(is_video, token * 4, -8)
    column = iota((rows, count), 1)
    source = iota((block, width), 0)
    place = iota((block, width), 1)
    total = jnp.zeros((rows, width), F32)
    for s in range(4):
        picked = dot_nt(one_hot(column == target + s), patch).astype(BF)
        total += dot(picked, one_hot(place == source + s * block))

    frames = mel_ref.shape[0] // 4
    wide_mel[...] = mel_ref[...].astype(F32)
    f0, f1, f2, f3 = (wide_mel[pl.ds(k, frames, stride=4), :] for k in range(4))
    shifted[0:1, :] = rim_ref[...].astype(F32)
    shifted[1:frames, :] = wide_mel[pl.ds(3, frames - 1, stride=4), :]
    before, f0, f1, f2, f3 = (f.astype(BF) for f in (shifted[...], f0, f1, f2, f3))
    c0, c1, c2 = (conv_ref[:, k * 128 : (k + 1) * 128] for k in range(3))
    even = dot_nt(before, c0) + dot_nt(f0, c1) + dot_nt(f1, c2)
    odd = dot_nt(f1, c0) + dot_nt(f2, c1) + dot_nt(f3, c2)
    pooled = (0.5 * (gelu(even) + gelu(odd))).astype(BF)
    column = iota((rows, frames), 1)
    start = start + of_kind(kept)
    for i in range(nx):
        index = jnp.minimum((i * nz + far - start) & (VT - 1), AT - 1) + kind * AT
        index = jnp.where(is_video | (kind >= spans), -8, index)
        picked = dot(one_hot(column == index), pooled).astype(BF)
        total += dot(picked, one_hot(place == source + i * block))
    out_ref[...] = total.astype(BF)


def vision_kernel(
    video_ref, audio_ref, up0, down0, up1, down1, send_ref, xs, wu, wd, sems
):
    copies = []
    for i, (u, d) in enumerate(((up0, down0), (up1, down1))):
        copies.append(pltpu.make_async_copy(u, wu.at[i], sems.at[2 * i]))
        copies.append(pltpu.make_async_copy(d, wd.at[i], sems.at[2 * i + 1]))
    for copy in copies:
        copy.start()
    ny, cores, half, width = video_ref.shape
    block = width // 4
    for y in range(ny):
        for c in range(cores):
            for s in range(4):
                a, b = (y * cores + c) * block, s * block
                xs[s * half : (s + 1) * half, a : a + block] = video_ref[y, c, :, b : b + block]
    wide = xs[...].astype(F32)
    centred = wide - jnp.mean(wide, axis=1, keepdims=True)
    spread = jnp.mean(centred * centred, axis=1, keepdims=True)
    normed = (centred * lax.rsqrt(spread + 1e-06)).astype(BF)
    total = None
    for i in range(2):
        copies[2 * i].wait()
        hidden = gelu(dot(normed, wu[i])).astype(BF)
        copies[2 * i + 1].wait()
        term = dot(hidden, wd[i])
        total = term if total is None else total + term
    total += wide * (1.0 / ny)
    parts = send_ref.shape[0] // 4
    some = half // parts
    send_ref[...] = jnp.zeros_like(send_ref)
    for s in range(4):
        for x in range(parts):
            a = s * half + x * some
            send_ref[x * ny + s, :some] = total[a : a + some].astype(BF)
            for c in range(cores):
                for k in range(3):
                    a, b = (c * 3 + k) * block, x * block
                    send_ref[x * ny + s, some:, a : a + block] = audio_ref[c, k, :, b : b + block]


def audio_kernel(in_ref, out_ref):
    ny, tokens, _ = out_ref.shape
    block, parts = in_ref.shape[2] // 8, in_ref.shape[0] // ny
    owners = tokens // 3
    near = owners // parts
    some = in_ref.shape[1] - near
    source, place = iota((block, 256), 0), iota((block, 256), 1)
    group = place // PAD_A
    lane = place - group * PAD_A
    spread = one_hot((lane < 20) & (source == group * 20 + lane))
    for y in range(ny):
        for c in range(2):
            for k in range(3):
                a = (c * 3 + k) * block
                rows = [in_ref[x * ny + y, some:, a : a + block] for x in range(parts)]
                piece = dot(jnp.concatenate(rows, axis=0), spread).astype(BF)
                out_ref[y, k * owners : (k + 1) * owners, c * 256 : (c + 1) * 256] = piece


def tail_kernel(
    own_ref,
    other_ref,
    audio_own_ref,
    audio_other_ref,
    low_ref,
    high_ref,
    place_ref,
    text_ref,
    out_ref,
    video,
    audio,
    spread,
    marks,
    text,
    sem,
):
    step = pl.program_id(0)
    fetch = pltpu.make_async_copy(text_ref, text, sem)

    @pl.when(step == 0)
    def _():
        fetch.start()
        video[...] = jnp.zeros_like(video)
        audio[...] = jnp.zeros_like(audio)
        spread[...] = jnp.zeros_like(spread)
        marks[...] = one_hot(place_ref[...] == iota(marks.shape, 0))

    near, _, rows, columns = low_ref.shape
    rows_a = rows // 5
    rows_m = rows - rows_a
    both = jnp.concatenate([own_ref[0], other_ref[0]], axis=0)
    depth = near * rows_m
    total = video[...]
    for i, ref in enumerate((low_ref, high_ref)):
        merge_w = ref[:, 0, :rows_m, :].reshape(depth, columns)
        total += dot(both[:, i * depth : (i + 1) * depth], merge_w)
        for z in range(near):
            a = (i * near + z) * PAD_A
            spread[a : a + rows_a, :] = ref[z, 0, rows_m:, :]
    video[...] = total
    tokens = jnp.concatenate([audio_own_ref[0], audio_other_ref[0]], axis=0)
    audio[...] += dot(tokens, spread[...])

    @pl.when(step == 3)
    def _():
        media = jnp.concatenate([video[...], audio[...]], axis=0).astype(BF)
        placed = lax.dot_general(
            media, marks[...], (((0,), (1,)), ((), ())), preferred_element_type=F32
        )
        taken = dot_nt(jnp.ones((8, media.shape[0]), BF), marks[...])[0:1, :]
        fetch.wait()
        out_ref[...] = jnp.where(taken > 0.5, placed, text[...].astype(F32)).astype(BF)


def local(
    mel_frames,
    conv_weight,
    patches,
    vit_up,
    vit_down,
    audio_proj,
    merger,
    text_rows,
    span_order,
    offsets,
    audio_count,
    video_count,
):
    nx, nz, ny = (lax.axis_size(a) for a in ("x", "z", "y"))
    owners = nx * nz
    position = lax.axis_index(TM)
    my_core = lax.axis_index("core")
    spans = mel_frames.shape[0] // (4 * AT)
    tokens = spans * owners
    half = tokens // 2
    columns, rows_m, rows_a = merger.shape[1], merger.shape[0], audio_proj.shape[0]
    rows_w = rows_m + rows_a
    width = 4 * patches.shape[1]
    full = vit_down.shape[1]

    rim = lax.ppermute(mel_frames[-1:], TM, [(i, i + 1) for i in range(owners - 1)])

    own = jnp.concatenate([merger, audio_proj], axis=0)
    everywhere = jnp.stack([own] * nx)
    rim, everywhere = lax.optimization_barrier((rim, everywhere))
    block = lax.all_to_all(everywhere, "x", 0, 0, tiled=True)

    starts = span_starts(span_order, offsets)
    prep_in = (
        span_order.reshape(1, -1),
        offsets.reshape(1, -1),
        video_count.reshape(1, -1),
        patches.T,
        mel_frames,
        rim,
        conv_weight.T,
    )
    outgoing = pl.pallas_call(
        prep_kernel,
        name="prep",
        out_shape=jax.ShapeDtypeStruct((nz * 16, width), BF),
        grid=(1,),
        in_specs=[whole(v.shape) for v in prep_in],
        out_specs=whole((nz * 16, width)),
        scratch_shapes=[
            pltpu.VMEM(mel_frames.shape, F32),
            pltpu.VMEM((spans * AT, mel_frames.shape[1]), F32),
        ],
        compiler_params=params(60),
        cost_estimate=pl.CostEstimate(
            flops=2000000000, bytes_accessed=8000000, transcendentals=500000
        ),
    )(*prep_in)
    block, outgoing = lax.optimization_barrier((block, outgoing))
    weights = lax.all_gather(block, "z", axis=0, tiled=False)
    arrived = lax.all_to_all(outgoing.reshape(nz, 16, width), "z", 0, 0, tiled=True)

    videos, half_z = nx * spans, nz // 2
    seq_count = text_rows.shape[0]
    video_where = jnp.mod(position - starts, owners)
    video_place = jnp.where(video_where < video_count, (starts + video_where) // owners, seq_count)
    audio_where = jnp.mod(position - starts - video_count, owners)
    audio_place = jnp.where(
        audio_where < audio_count, (starts + video_count + audio_where) // owners, seq_count
    )


    def ordered(places, axes):
        places = places.reshape(nx, 2, half_z, spans)
        places = jnp.where(my_core == 0, places, places[:, ::-1])
        return jnp.transpose(places, axes).reshape(-1)

    video_place = ordered(video_place, (1, 0, 2, 3))
    audio_place = ordered(audio_place, (1, 3, 0, 2))
    places = jnp.concatenate([video_place, audio_place])
    text = text_rows[:, 0, :].T

    arrived, places = lax.optimization_barrier((arrived, places.reshape(1, -1)))

    up_other, down_other = swap(vit_up), swap(vit_down)
    cores = lax.all_gather(arrived, "core", axis=0, tiled=False)
    near = lax.dynamic_slice_in_dim(cores, my_core * half_z, half_z, axis=1)
    pair = near[:, :, :videos].reshape(2, half_z, nx, spans, width)
    video_pair = jnp.transpose(pair, (0, 2, 1, 3, 4)).reshape(2, half, width)
    video_y = lax.all_gather(video_pair, "y", axis=0, tiled=False)
    audio_own = jnp.transpose(near[:, :, videos : videos + spans], (0, 2, 1, 3))

    some = half // nx
    rows_sent = some + half_z
    flops = 2 * 4 * half * full * 4 * vit_up.shape[1]
    partial_sum = pl.pallas_call(
        vision_kernel,
        name="vision",
        out_shape=jax.ShapeDtypeStruct((nx * ny, rows_sent, full), BF),
        in_specs=[VMEM, VMEM, ANY, ANY, ANY, ANY],
        out_specs=VMEM,
        scratch_shapes=[
            pltpu.VMEM((4 * half, full), BF),
            pltpu.VMEM((2,) + vit_up.shape, BF),
            pltpu.VMEM((2,) + vit_down.shape, BF),
            pltpu.SemaphoreType.DMA((4,)),
        ],
        compiler_params=params(28),
        cost_estimate=pl.CostEstimate(flops=flops, bytes_accessed=9000000, transcendentals=500000),
    )(video_y, audio_own, vit_up, vit_down, up_other, down_other)

    incoming = lax.all_to_all(partial_sum, ("x", "y"), 0, 0, tiled=True)
    audio_tokens = pl.pallas_call(
        audio_kernel,
        name="audio_spread",
        out_shape=jax.ShapeDtypeStruct((ny, half, nz * PAD_A), BF),
        in_specs=[VMEM],
        out_specs=VMEM,
        compiler_params=params(8),
    )(incoming)
    audio_theirs = swap(audio_tokens)
    summed = jnp.sum(incoming.reshape(nx, ny, rows_sent, full)[:, :, :some].astype(F32), axis=1)
    vit_out = summed.astype(BF).reshape(half, full)
    vit_mine = lax.all_gather(vit_out, "y", axis=0, tiled=False)
    vit_theirs = swap(vit_mine)

    result = pl.pallas_call(
        tail_kernel,
        name="project_place",
        out_shape=jax.ShapeDtypeStruct((columns, seq_count), BF),
        grid_spec=pl.GridSpec(
            grid=(nx,),
            in_specs=[
                pl.BlockSpec((1, half, full), lambda s: (s, 0, 0)),
                pl.BlockSpec((1, half, full), lambda s: (s, 0, 0)),
                pl.BlockSpec((1, half, nz * PAD_A), lambda s: (s, 0, 0)),
                pl.BlockSpec((1, half, nz * PAD_A), lambda s: (s, 0, 0)),
                pl.BlockSpec((half_z, 1, rows_w, columns), lambda s: (0, s, 0, 0)),
                pl.BlockSpec((half_z, 1, rows_w, columns), lambda s: (1, s, 0, 0)),
                whole((1, 2 * tokens)),
                ANY,
            ],
            out_specs=whole((columns, seq_count)),
            scratch_shapes=[
                pltpu.VMEM((tokens, columns), F32),
                pltpu.VMEM((tokens, columns), F32),
                pltpu.VMEM((nz * PAD_A, columns), BF),
                pltpu.VMEM((seq_count, 2 * tokens), BF),
                pltpu.VMEM((columns, seq_count), BF),
                pltpu.SemaphoreType.DMA,
            ],
        ),
        compiler_params=params(48),
        cost_estimate=pl.CostEstimate(flops=1100000000, bytes_accessed=9000000, transcendentals=0),
    )(
        vit_mine,
        vit_theirs,
        audio_tokens,
        audio_theirs,
        weights.reshape(nz, nx, rows_w, columns),
        weights.reshape(nz, nx, rows_w, columns),
        places,
        text,
    )
    return result.T[:, None, :]


def solution(mesh):
    grid = Mesh(mesh.devices.reshape(4, 16, 4, 2), ("x", "z", "y", "core"))
    placed = (
        P(TM, None),
        P(None, MP),
        P(TM, MP),
        P(None, MP),
        P(MP, None),
        P(TM, MP),
        P(TM, MP),
        P(None, TM, MP),
        P(),
        P(),
        P(),
        P(),
    )
    return jax.shard_map(
        local, mesh=grid, in_specs=placed, out_specs=P(None, TM, MP), check_vma=False
    )
```

```python
import jax
import jax.numpy as jnp
from jax import lax
from jax.experimental import pallas as pl
from jax.experimental.pallas import tpu as pltpu
from jax.sharding import Mesh, PartitionSpec as P

AT = 50
VT = 64
BF = jnp.bfloat16
F32 = jnp.float32
I32 = jnp.int32
TM = ("x", "z")
MP = ("y", "core")
PAD_A = 32
VMEM = pl.BlockSpec(memory_space=pltpu.VMEM)
SMEM = pl.BlockSpec(memory_space=pltpu.SMEM)
ANY = pl.BlockSpec(memory_space=pl.ANY)
ROOT_HALF = 0.7071067811865476


def span_starts(span_order, offsets):
    listed = jnp.arange(span_order.shape[0], dtype=I32)
    matches = (span_order[:, None] == listed[None, :]).astype(I32)
    return jnp.sum(matches * offsets[:, None], axis=0)


def ring(value, axis, step):
    count = lax.axis_size(axis)
    return lax.ppermute(value, axis, [(i, (i + step) % count) for i in range(count)])


def swap(value):
    return lax.ppermute(value, "core", [(0, 1), (1, 0)])


def gelu(value):
    return 0.5 * value * (1.0 + lax.erf(value * ROOT_HALF))


def dot(a, b):
    return jnp.dot(a, b, preferred_element_type=F32)


def dot_nt(a, b):
    return lax.dot_general(a, b, (((1,), (1,)), ((), ())), preferred_element_type=F32)


def iota(shape, axis):
    return lax.broadcasted_iota(I32, shape, axis)


def params(mib):
    return pltpu.CompilerParams(vmem_limit_bytes=mib * 1024 * 1024)


def whole(shape):
    return pl.BlockSpec(shape, lambda *i: (0,) * len(shape))


def one_hot(condition):
    return jnp.where(condition, 1.0, 0.0).astype(BF)


def prep_kernel(
    order_ref, offset_ref, video_ref, patch_ref, mel_ref, rim_ref, conv_ref, out_ref, wide_mel, shifted
):
    rows, width = out_ref.shape
    spans, count = 3, patch_ref.shape[1]
    block = patch_ref.shape[0]
    nx, nz = lax.axis_size("x"), lax.axis_size("z")
    videos = nx * spans
    position = lax.axis_index("x") * lax.axis_size("z") + lax.axis_index("z")
    listed = iota(order_ref.shape, 1)

    def pick(condition, values):
        return jnp.sum(jnp.where(condition, values, 0), axis=1, keepdims=True)

    first = [pick(order_ref[...] == position * spans + k, offset_ref[...]) for k in range(spans)]
    kept = [pick(listed == position * spans + k, video_ref[...]) for k in range(spans)]
    patch = patch_ref[...]
    row = iota((rows, 1), 0)
    far, slot = row >> 4, row & 15
    to_x = sum((slot >= spans * i).astype(I32) for i in range(1, nx))
    is_video = slot < videos
    kind = jnp.where(is_video, slot - spans * to_x, slot - videos)

    def of_kind(values):
        return jnp.where(kind == 0, values[0], jnp.where(kind == 1, values[1], values[2]))

    start = of_kind(first)
    token = (kind << 6) + ((to_x * nz + far - start) & (VT - 1))
    target = jnp.where(is_video, token * 4, -8)
    frames = mel_ref.shape[0] // 4
    wide_mel[...] = mel_ref[...].astype(F32)
    f0, f1, f2, f3 = (wide_mel[pl.ds(k, frames, stride=4), :] for k in range(4))
    shifted[0:1, :] = rim_ref[...].astype(F32)
    shifted[1:frames, :] = wide_mel[pl.ds(3, frames - 1, stride=4), :]
    before, f0, f1, f2, f3 = (f.astype(BF) for f in (shifted[...], f0, f1, f2, f3))
    c0, c1, c2 = (conv_ref[:, k * 128 : (k + 1) * 128] for k in range(3))
    even = dot_nt(before, c0) + dot_nt(f0, c1) + dot_nt(f1, c2)
    odd = dot_nt(f1, c0) + dot_nt(f2, c1) + dot_nt(f3, c2)
    pooled = (0.5 * (gelu(even) + gelu(odd))).astype(BF)
    start = start + of_kind(kept)
    is_audio = (slot >= videos) & (kind < spans)
    patch_column, column = iota((rows, count), 1), iota((rows, frames), 1)
    for i in range(nx):
        index = jnp.minimum((i * nz + far - start) & (VT - 1), AT - 1) + kind * AT
        index = jnp.where(is_audio, index, -8)
        video = dot_nt(one_hot(patch_column == target + i), patch)
        audio = dot(one_hot(column == index), pooled)
        out_ref[:, i * block : (i + 1) * block] = (video + audio).astype(BF)


def vision_kernel(
    video_ref, audio_ref, up0, down0, up1, down1, send_ref, xs, wu, wd, sems
):
    copies = []
    for i, (u, d) in enumerate(((up0, down0), (up1, down1))):
        copies.append(pltpu.make_async_copy(u, wu.at[i], sems.at[2 * i]))
        copies.append(pltpu.make_async_copy(d, wd.at[i], sems.at[2 * i + 1]))
    for copy in copies:
        copy.start()
    ny, cores, half, width = video_ref.shape
    block = width // 4
    for y in range(ny):
        for c in range(cores):
            for s in range(4):
                a, b = (y * cores + c) * block, s * block
                xs[s * half : (s + 1) * half, a : a + block] = video_ref[y, c, :, b : b + block]
    wide = xs[...].astype(F32)
    centred = wide - jnp.mean(wide, axis=1, keepdims=True)
    spread = jnp.mean(centred * centred, axis=1, keepdims=True)
    normed = (centred * lax.rsqrt(spread + 1e-06)).astype(BF)
    total = None
    for i in range(2):
        copies[2 * i].wait()
        hidden = gelu(dot(normed, wu[i])).astype(BF)
        copies[2 * i + 1].wait()
        term = dot(hidden, wd[i])
        total = term if total is None else total + term
    total += wide * (1.0 / ny)
    parts = send_ref.shape[0] // 4
    some = half // parts
    send_ref[...] = jnp.zeros_like(send_ref)
    for s in range(4):
        for x in range(parts):
            a = s * half + x * some
            send_ref[x * ny + s, :some] = total[a : a + some].astype(BF)
            for c in range(cores):
                for k in range(3):
                    a, b = (c * 3 + k) * block, x * block
                    send_ref[x * ny + s, some:, a : a + block] = audio_ref[c, k, :, b : b + block]


def audio_kernel(in_ref, out_ref):
    ny, tokens, _ = out_ref.shape
    block, parts = in_ref.shape[2] // 8, in_ref.shape[0] // ny
    owners = tokens // 3
    near = owners // parts
    some = in_ref.shape[1] - near
    source, place = iota((block, 256), 0), iota((block, 256), 1)
    group = place // PAD_A
    lane = place - group * PAD_A
    spread = one_hot((lane < 20) & (source == group * 20 + lane))
    for y in range(ny):
        for c in range(2):
            for k in range(3):
                a = (c * 3 + k) * block
                rows = [in_ref[x * ny + y, some:, a : a + block] for x in range(parts)]
                piece = dot(jnp.concatenate(rows, axis=0), spread).astype(BF)
                out_ref[y, k * owners : (k + 1) * owners, c * 256 : (c + 1) * 256] = piece


def tail_kernel(
    own_ref,
    other_ref,
    audio_own_ref,
    audio_other_ref,
    low_ref,
    high_ref,
    place_ref,
    text_ref,
    out_ref,
    video,
    audio,
    spread,
    marks,
    text,
    sem,
):
    step = pl.program_id(0)
    fetch = pltpu.make_async_copy(text_ref, text, sem)

    @pl.when(step == 0)
    def _():
        fetch.start()
        video[...] = jnp.zeros_like(video)
        audio[...] = jnp.zeros_like(audio)
        spread[...] = jnp.zeros_like(spread)
        marks[...] = one_hot(place_ref[...] == iota(marks.shape, 0))

    near, _, rows, columns = low_ref.shape
    rows_a = rows // 5
    rows_m = rows - rows_a
    both = jnp.concatenate([own_ref[0], other_ref[0]], axis=0)
    depth = near * rows_m
    total = video[...]
    for i, ref in enumerate((low_ref, high_ref)):
        merge_w = ref[:, 0, :rows_m, :].reshape(depth, columns)
        total += dot(both[:, i * depth : (i + 1) * depth], merge_w)
        for z in range(near):
            a = (i * near + z) * PAD_A
            spread[a : a + rows_a, :] = ref[z, 0, rows_m:, :]
    video[...] = total
    tokens = jnp.concatenate([audio_own_ref[0], audio_other_ref[0]], axis=0)
    audio[...] += dot(tokens, spread[...])

    @pl.when(step == 3)
    def _():
        media = jnp.concatenate([video[...], audio[...]], axis=0).astype(BF)
        placed = lax.dot_general(
            media, marks[...], (((0,), (1,)), ((), ())), preferred_element_type=F32
        )
        taken = dot_nt(jnp.ones((8, media.shape[0]), BF), marks[...])[0:1, :]
        fetch.wait()
        out_ref[...] = jnp.where(taken > 0.5, placed, text[...].astype(F32)).astype(BF)


def local(
    mel_frames,
    conv_weight,
    patches,
    vit_up,
    vit_down,
    audio_proj,
    merger,
    text_rows,
    span_order,
    offsets,
    audio_count,
    video_count,
):
    nx, nz, ny = (lax.axis_size(a) for a in ("x", "z", "y"))
    owners = nx * nz
    position = lax.axis_index(TM)
    my_core = lax.axis_index("core")
    spans = mel_frames.shape[0] // (4 * AT)
    tokens = spans * owners
    half = tokens // 2
    columns, rows_m, rows_a = merger.shape[1], merger.shape[0], audio_proj.shape[0]
    rows_w = rows_m + rows_a
    width = 4 * patches.shape[1]
    full = vit_down.shape[1]

    rim = lax.ppermute(mel_frames[-1:], TM, [(i, i + 1) for i in range(owners - 1)])

    own = jnp.concatenate([merger, audio_proj], axis=0)
    everywhere = jnp.stack([own] * nx)
    rim, everywhere = lax.optimization_barrier((rim, everywhere))
    block = lax.all_to_all(everywhere, "x", 0, 0, tiled=True)

    starts = span_starts(span_order, offsets)
    prep_in = (
        span_order.reshape(1, -1),
        offsets.reshape(1, -1),
        video_count.reshape(1, -1),
        patches.T,
        mel_frames,
        rim,
        conv_weight.T,
    )
    outgoing = pl.pallas_call(
        prep_kernel,
        name="prep",
        out_shape=jax.ShapeDtypeStruct((nz * 16, width), BF),
        grid=(1,),
        in_specs=[whole(v.shape) for v in prep_in],
        out_specs=whole((nz * 16, width)),
        scratch_shapes=[
            pltpu.VMEM(mel_frames.shape, F32),
            pltpu.VMEM((spans * AT, mel_frames.shape[1]), F32),
        ],
        compiler_params=params(60),
        cost_estimate=pl.CostEstimate(
            flops=2000000000, bytes_accessed=8000000, transcendentals=500000
        ),
    )(*prep_in)
    block, outgoing = lax.optimization_barrier((block, outgoing))
    weights = lax.all_gather(block, "z", axis=0, tiled=False)
    arrived = lax.all_to_all(outgoing.reshape(nz, 16, width), "z", 0, 0, tiled=True)

    videos, half_z = nx * spans, nz // 2
    seq_count = text_rows.shape[0]
    video_where = jnp.mod(position - starts, owners)
    video_place = jnp.where(video_where < video_count, (starts + video_where) // owners, seq_count)
    audio_where = jnp.mod(position - starts - video_count, owners)
    audio_place = jnp.where(
        audio_where < audio_count, (starts + video_count + audio_where) // owners, seq_count
    )


    def ordered(places, axes):
        places = places.reshape(nx, 2, half_z, spans)
        places = jnp.where(my_core == 0, places, places[:, ::-1])
        return jnp.transpose(places, axes).reshape(-1)

    video_place = ordered(video_place, (1, 0, 2, 3))
    audio_place = ordered(audio_place, (1, 3, 0, 2))
    places = jnp.concatenate([video_place, audio_place])
    text = text_rows[:, 0, :].T

    arrived, places = lax.optimization_barrier((arrived, places.reshape(1, -1)))

    up_other, down_other = swap(vit_up), swap(vit_down)
    cores = lax.all_gather(arrived, "core", axis=0, tiled=False)
    near = lax.dynamic_slice_in_dim(cores, my_core * half_z, half_z, axis=1)
    pair = near[:, :, :videos].reshape(2, half_z, nx, spans, width)
    video_pair = jnp.transpose(pair, (0, 2, 1, 3, 4)).reshape(2, half, width)
    video_y = lax.all_gather(video_pair, "y", axis=0, tiled=False)
    audio_own = jnp.transpose(near[:, :, videos : videos + spans], (0, 2, 1, 3))

    some = half // nx
    rows_sent = some + half_z
    flops = 2 * 4 * half * full * 4 * vit_up.shape[1]
    partial_sum = pl.pallas_call(
        vision_kernel,
        name="vision",
        out_shape=jax.ShapeDtypeStruct((nx * ny, rows_sent, full), BF),
        in_specs=[VMEM, VMEM, ANY, ANY, ANY, ANY],
        out_specs=VMEM,
        scratch_shapes=[
            pltpu.VMEM((4 * half, full), BF),
            pltpu.VMEM((2,) + vit_up.shape, BF),
            pltpu.VMEM((2,) + vit_down.shape, BF),
            pltpu.SemaphoreType.DMA((4,)),
        ],
        compiler_params=params(28),
        cost_estimate=pl.CostEstimate(flops=flops, bytes_accessed=9000000, transcendentals=500000),
    )(video_y, audio_own, vit_up, vit_down, up_other, down_other)

    incoming = lax.all_to_all(partial_sum, ("x", "y"), 0, 0, tiled=True)
    audio_tokens = pl.pallas_call(
        audio_kernel,
        name="audio_spread",
        out_shape=jax.ShapeDtypeStruct((ny, half, nz * PAD_A), BF),
        in_specs=[VMEM],
        out_specs=VMEM,
        compiler_params=params(8),
    )(incoming)
    audio_theirs = swap(audio_tokens)
    summed = jnp.sum(incoming.reshape(nx, ny, rows_sent, full)[:, :, :some].astype(F32), axis=1)
    vit_out = summed.astype(BF).reshape(half, full)
    vit_mine = lax.all_gather(vit_out, "y", axis=0, tiled=False)
    vit_theirs = swap(vit_mine)

    result = pl.pallas_call(
        tail_kernel,
        name="project_place",
        out_shape=jax.ShapeDtypeStruct((columns, seq_count), BF),
        grid_spec=pl.GridSpec(
            grid=(nx,),
            in_specs=[
                pl.BlockSpec((1, half, full), lambda s: (s, 0, 0)),
                pl.BlockSpec((1, half, full), lambda s: (s, 0, 0)),
                pl.BlockSpec((1, half, nz * PAD_A), lambda s: (s, 0, 0)),
                pl.BlockSpec((1, half, nz * PAD_A), lambda s: (s, 0, 0)),
                pl.BlockSpec((half_z, 1, rows_w, columns), lambda s: (0, s, 0, 0)),
                pl.BlockSpec((half_z, 1, rows_w, columns), lambda s: (1, s, 0, 0)),
                whole((1, 2 * tokens)),
                ANY,
            ],
            out_specs=whole((columns, seq_count)),
            scratch_shapes=[
                pltpu.VMEM((tokens, columns), F32),
                pltpu.VMEM((tokens, columns), F32),
                pltpu.VMEM((nz * PAD_A, columns), BF),
                pltpu.VMEM((seq_count, 2 * tokens), BF),
                pltpu.VMEM((columns, seq_count), BF),
                pltpu.SemaphoreType.DMA,
            ],
        ),
        compiler_params=params(48),
        cost_estimate=pl.CostEstimate(flops=1100000000, bytes_accessed=9000000, transcendentals=0),
    )(
        vit_mine,
        vit_theirs,
        audio_tokens,
        audio_theirs,
        weights.reshape(nz, nx, rows_w, columns),
        weights.reshape(nz, nx, rows_w, columns),
        places,
        text,
    )
    return result.T[:, None, :]


def solution(mesh):
    grid = Mesh(mesh.devices.reshape(4, 16, 4, 2), ("x", "z", "y", "core"))
    placed = (
        P(TM, None),
        P(None, MP),
        P(TM, MP),
        P(None, MP),
        P(MP, None),
        P(TM, MP),
        P(TM, MP),
        P(None, TM, MP),
        P(),
        P(),
        P(),
        P(),
    )
    return jax.shard_map(
        local, mesh=grid, in_specs=placed, out_specs=P(None, TM, MP), check_vma=False
    )
```

```python
import jax
import jax.numpy as jnp
from jax import lax
from jax.experimental import pallas as pl
from jax.experimental.pallas import tpu as pltpu
from jax.sharding import Mesh, PartitionSpec as P

AT = 50
VT = 64
BF = jnp.bfloat16
F32 = jnp.float32
I32 = jnp.int32
TM = ("x", "z")
MP = ("y", "core")
PAD_A = 32
VMEM = pl.BlockSpec(memory_space=pltpu.VMEM)
SMEM = pl.BlockSpec(memory_space=pltpu.SMEM)
ANY = pl.BlockSpec(memory_space=pl.ANY)
ROOT_HALF = 0.7071067811865476


def span_starts(span_order, offsets):
    listed = jnp.arange(span_order.shape[0], dtype=I32)
    matches = (span_order[:, None] == listed[None, :]).astype(I32)
    return jnp.sum(matches * offsets[:, None], axis=0)


def ring(value, axis, step):
    count = lax.axis_size(axis)
    return lax.ppermute(value, axis, [(i, (i + step) % count) for i in range(count)])


def swap(value):
    return lax.ppermute(value, "core", [(0, 1), (1, 0)])


def gelu(value):
    return 0.5 * value * (1.0 + lax.erf(value * ROOT_HALF))


def dot(a, b):
    return jnp.dot(a, b, preferred_element_type=F32)


def dot_nt(a, b):
    return lax.dot_general(a, b, (((1,), (1,)), ((), ())), preferred_element_type=F32)


def iota(shape, axis):
    return lax.broadcasted_iota(I32, shape, axis)


def params(mib):
    return pltpu.CompilerParams(vmem_limit_bytes=mib * 1024 * 1024)


def whole(shape):
    return pl.BlockSpec(shape, lambda *i: (0,) * len(shape))


def one_hot(condition):
    return jnp.where(condition, 1.0, 0.0).astype(BF)


def prep_kernel(
    order_ref, offset_ref, video_ref, patch_ref, mel_ref, rim_ref, conv_ref, out_ref, wide_mel, shifted
):
    rows, width = out_ref.shape
    spans, count = 3, patch_ref.shape[1]
    block = patch_ref.shape[0]
    nx, nz = lax.axis_size("x"), lax.axis_size("z")
    videos = nx * spans
    position = lax.axis_index("x") * lax.axis_size("z") + lax.axis_index("z")
    listed = iota(order_ref.shape, 1)

    def pick(condition, values):
        return jnp.sum(jnp.where(condition, values, 0), axis=1, keepdims=True)

    first = [pick(order_ref[...] == position * spans + k, offset_ref[...]) for k in range(spans)]
    kept = [pick(listed == position * spans + k, video_ref[...]) for k in range(spans)]
    patch = patch_ref[...]
    row = iota((rows, 1), 0)
    far, slot = row >> 4, row & 15
    to_x = sum((slot >= spans * i).astype(I32) for i in range(1, nx))
    is_video = slot < videos
    kind = jnp.where(is_video, slot - spans * to_x, slot - videos)

    def of_kind(values):
        return jnp.where(kind == 0, values[0], jnp.where(kind == 1, values[1], values[2]))

    start = of_kind(first)
    token = (kind << 6) + ((to_x * nz + far - start) & (VT - 1))
    target = jnp.where(is_video, token * 4, -8)
    frames = mel_ref.shape[0] // 4
    wide_mel[...] = mel_ref[...].astype(F32)
    f0, f1, f2, f3 = (wide_mel[pl.ds(k, frames, stride=4), :] for k in range(4))
    shifted[0:1, :] = rim_ref[...].astype(F32)
    shifted[1:frames, :] = wide_mel[pl.ds(3, frames - 1, stride=4), :]
    before, f0, f1, f2, f3 = (f.astype(BF) for f in (shifted[...], f0, f1, f2, f3))
    c0, c1, c2 = (conv_ref[:, k * 128 : (k + 1) * 128] for k in range(3))
    even = dot_nt(before, c0) + dot_nt(f0, c1) + dot_nt(f1, c2)
    odd = dot_nt(f1, c0) + dot_nt(f2, c1) + dot_nt(f3, c2)
    pooled = (0.5 * (gelu(even) + gelu(odd))).astype(BF)
    start = start + of_kind(kept)
    is_audio = (slot >= videos) & (kind < spans)
    patch_column, column = iota((rows, count), 1), iota((rows, frames), 1)
    for i in range(nx):
        index = jnp.minimum((i * nz + far - start) & (VT - 1), AT - 1) + kind * AT
        index = jnp.where(is_audio, index, -8)
        video = dot_nt(one_hot(patch_column == target + i), patch)
        audio = dot(one_hot(column == index), pooled)
        out_ref[:, i * block : (i + 1) * block] = (video + audio).astype(BF)


def vision_kernel(
    video_ref, audio_ref, up0, down0, up1, down1, send_ref, xs, wu, wd, sems
):
    copies = []
    for i, (u, d) in enumerate(((up0, down0), (up1, down1))):
        copies.append(pltpu.make_async_copy(u, wu.at[i], sems.at[2 * i]))
        copies.append(pltpu.make_async_copy(d, wd.at[i], sems.at[2 * i + 1]))
    for copy in copies:
        copy.start()
    ny, cores, half, width = video_ref.shape
    block = width // 4
    for y in range(ny):
        for c in range(cores):
            for s in range(4):
                a, b = (y * cores + c) * block, s * block
                xs[s * half : (s + 1) * half, a : a + block] = video_ref[y, c, :, b : b + block]
    wide = xs[...].astype(F32)
    centred = wide - jnp.mean(wide, axis=1, keepdims=True)
    spread = jnp.mean(centred * centred, axis=1, keepdims=True)
    normed = (centred * lax.rsqrt(spread + 1e-06)).astype(BF)
    total = None
    for i in range(2):
        copies[2 * i].wait()
        hidden = gelu(dot(normed, wu[i])).astype(BF)
        copies[2 * i + 1].wait()
        term = dot(hidden, wd[i])
        total = term if total is None else total + term
    total += wide * (1.0 / ny)
    parts = send_ref.shape[0] // 4
    some = half // parts
    send_ref[...] = jnp.zeros_like(send_ref)
    for s in range(4):
        for x in range(parts):
            a = s * half + x * some
            send_ref[x * ny + s, :some] = total[a : a + some].astype(BF)
            for c in range(cores):
                for k in range(3):
                    a, b = (c * 3 + k) * block, x * block
                    send_ref[x * ny + s, some:, a : a + block] = audio_ref[c, k, :, b : b + block]


def audio_kernel(in_ref, out_ref):
    ny, tokens, _ = out_ref.shape
    block, parts = in_ref.shape[2] // 8, in_ref.shape[0] // ny
    owners = tokens // 3
    near = owners // parts
    some = in_ref.shape[1] - near
    source, place = iota((block, 256), 0), iota((block, 256), 1)
    group = place // PAD_A
    lane = place - group * PAD_A
    spread = one_hot((lane < 20) & (source == group * 20 + lane))
    for y in range(ny):
        for c in range(2):
            for k in range(3):
                a = (c * 3 + k) * block
                rows = [in_ref[x * ny + y, some:, a : a + block] for x in range(parts)]
                piece = dot(jnp.concatenate(rows, axis=0), spread).astype(BF)
                out_ref[y, k * owners : (k + 1) * owners, c * 256 : (c + 1) * 256] = piece


def tail_kernel(
    own_ref,
    other_ref,
    audio_own_ref,
    audio_other_ref,
    low_ref,
    high_ref,
    place_ref,
    text_ref,
    out_ref,
    video,
    audio,
    spread,
    marks,
    text,
    sem,
):
    step = pl.program_id(0)
    fetch = pltpu.make_async_copy(text_ref, text, sem)

    @pl.when(step == 0)
    def _():
        fetch.start()
        video[...] = jnp.zeros_like(video)
        audio[...] = jnp.zeros_like(audio)
        spread[...] = jnp.zeros_like(spread)
        marks[...] = one_hot(place_ref[...] == iota(marks.shape, 0))

    near, _, rows, columns = low_ref.shape
    rows_a = rows // 5
    rows_m = rows - rows_a
    both = jnp.concatenate([own_ref[0], other_ref[0]], axis=0)
    depth = near * rows_m
    total = video[...]
    for i, ref in enumerate((low_ref, high_ref)):
        merge_w = ref[:, 0, :rows_m, :].reshape(depth, columns)
        total += dot(both[:, i * depth : (i + 1) * depth], merge_w)
        for z in range(near):
            a = (i * near + z) * PAD_A
            spread[a : a + rows_a, :] = ref[z, 0, rows_m:, :]
    video[...] = total
    tokens = jnp.concatenate([audio_own_ref[0], audio_other_ref[0]], axis=0)
    audio[...] += dot(tokens, spread[...])

    @pl.when(step == 3)
    def _():
        media = jnp.concatenate([video[...], audio[...]], axis=0).astype(BF)
        placed = lax.dot_general(
            media, marks[...], (((0,), (1,)), ((), ())), preferred_element_type=F32
        )
        taken = dot_nt(jnp.ones((8, media.shape[0]), BF), marks[...])[0:1, :]
        fetch.wait()
        out_ref[...] = jnp.where(taken > 0.5, placed, text[...].astype(F32)).astype(BF)


def local(
    mel_frames,
    conv_weight,
    patches,
    vit_up,
    vit_down,
    audio_proj,
    merger,
    text_rows,
    span_order,
    offsets,
    audio_count,
    video_count,
):
    nx, nz, ny = (lax.axis_size(a) for a in ("x", "z", "y"))
    owners = nx * nz
    position = lax.axis_index(TM)
    my_core = lax.axis_index("core")
    spans = mel_frames.shape[0] // (4 * AT)
    tokens = spans * owners
    half = tokens // 2
    columns, rows_m, rows_a = merger.shape[1], merger.shape[0], audio_proj.shape[0]
    rows_w = rows_m + rows_a
    width = 4 * patches.shape[1]
    full = vit_down.shape[1]

    rim = lax.ppermute(mel_frames[-1:], TM, [(i, i + 1) for i in range(owners - 1)])

    own = jnp.concatenate([merger, audio_proj], axis=0)
    everywhere = jnp.stack([own] * nx)
    block = lax.all_to_all(everywhere, "x", 0, 0, tiled=True)

    starts = span_starts(span_order, offsets)
    prep_in = (
        span_order.reshape(1, -1),
        offsets.reshape(1, -1),
        video_count.reshape(1, -1),
        patches.T,
        mel_frames,
        rim,
        conv_weight.T,
    )
    outgoing = pl.pallas_call(
        prep_kernel,
        name="prep",
        out_shape=jax.ShapeDtypeStruct((nz * 16, width), BF),
        grid=(1,),
        in_specs=[whole(v.shape) for v in prep_in],
        out_specs=whole((nz * 16, width)),
        scratch_shapes=[
            pltpu.VMEM(mel_frames.shape, F32),
            pltpu.VMEM((spans * AT, mel_frames.shape[1]), F32),
        ],
        compiler_params=params(60),
        cost_estimate=pl.CostEstimate(
            flops=2000000000, bytes_accessed=8000000, transcendentals=500000
        ),
    )(*prep_in)
    block, outgoing = lax.optimization_barrier((block, outgoing))
    weights = lax.all_gather(block, "z", axis=0, tiled=False)
    arrived = lax.all_to_all(outgoing.reshape(nz, 16, width), "z", 0, 0, tiled=True)

    videos, half_z = nx * spans, nz // 2
    seq_count = text_rows.shape[0]
    video_where = jnp.mod(position - starts, owners)
    video_place = jnp.where(video_where < video_count, (starts + video_where) // owners, seq_count)
    audio_where = jnp.mod(position - starts - video_count, owners)
    audio_place = jnp.where(
        audio_where < audio_count, (starts + video_count + audio_where) // owners, seq_count
    )


    def ordered(places, axes):
        places = places.reshape(nx, 2, half_z, spans)
        places = jnp.where(my_core == 0, places, places[:, ::-1])
        return jnp.transpose(places, axes).reshape(-1)

    video_place = ordered(video_place, (1, 0, 2, 3))
    audio_place = ordered(audio_place, (1, 3, 0, 2))
    places = jnp.concatenate([video_place, audio_place])
    text = text_rows[:, 0, :].T

    arrived, places = lax.optimization_barrier((arrived, places.reshape(1, -1)))

    up_other, down_other = swap(vit_up), swap(vit_down)
    cores = lax.all_gather(arrived, "core", axis=0, tiled=False)
    near = lax.dynamic_slice_in_dim(cores, my_core * half_z, half_z, axis=1)
    pair = near[:, :, :videos].reshape(2, half_z, nx, spans, width)
    video_pair = jnp.transpose(pair, (0, 2, 1, 3, 4)).reshape(2, half, width)
    video_y = lax.all_gather(video_pair, "y", axis=0, tiled=False)
    audio_own = jnp.transpose(near[:, :, videos : videos + spans], (0, 2, 1, 3))

    some = half // nx
    rows_sent = some + half_z
    flops = 2 * 4 * half * full * 4 * vit_up.shape[1]
    partial_sum = pl.pallas_call(
        vision_kernel,
        name="vision",
        out_shape=jax.ShapeDtypeStruct((nx * ny, rows_sent, full), BF),
        in_specs=[VMEM, VMEM, ANY, ANY, ANY, ANY],
        out_specs=VMEM,
        scratch_shapes=[
            pltpu.VMEM((4 * half, full), BF),
            pltpu.VMEM((2,) + vit_up.shape, BF),
            pltpu.VMEM((2,) + vit_down.shape, BF),
            pltpu.SemaphoreType.DMA((4,)),
        ],
        compiler_params=params(28),
        cost_estimate=pl.CostEstimate(flops=flops, bytes_accessed=9000000, transcendentals=500000),
    )(video_y, audio_own, vit_up, vit_down, up_other, down_other)

    incoming = lax.all_to_all(partial_sum, ("x", "y"), 0, 0, tiled=True)
    audio_tokens = pl.pallas_call(
        audio_kernel,
        name="audio_spread",
        out_shape=jax.ShapeDtypeStruct((ny, half, nz * PAD_A), BF),
        in_specs=[VMEM],
        out_specs=VMEM,
        compiler_params=params(8),
    )(incoming)
    audio_theirs = swap(audio_tokens)
    summed = jnp.sum(incoming.reshape(nx, ny, rows_sent, full)[:, :, :some].astype(F32), axis=1)
    vit_out = summed.astype(BF).reshape(half, full)
    vit_mine = lax.all_gather(vit_out, "y", axis=0, tiled=False)
    vit_theirs = swap(vit_mine)

    result = pl.pallas_call(
        tail_kernel,
        name="project_place",
        out_shape=jax.ShapeDtypeStruct((columns, seq_count), BF),
        grid_spec=pl.GridSpec(
            grid=(nx,),
            in_specs=[
                pl.BlockSpec((1, half, full), lambda s: (s, 0, 0)),
                pl.BlockSpec((1, half, full), lambda s: (s, 0, 0)),
                pl.BlockSpec((1, half, nz * PAD_A), lambda s: (s, 0, 0)),
                pl.BlockSpec((1, half, nz * PAD_A), lambda s: (s, 0, 0)),
                pl.BlockSpec((half_z, 1, rows_w, columns), lambda s: (0, s, 0, 0)),
                pl.BlockSpec((half_z, 1, rows_w, columns), lambda s: (1, s, 0, 0)),
                whole((1, 2 * tokens)),
                ANY,
            ],
            out_specs=whole((columns, seq_count)),
            scratch_shapes=[
                pltpu.VMEM((tokens, columns), F32),
                pltpu.VMEM((tokens, columns), F32),
                pltpu.VMEM((nz * PAD_A, columns), BF),
                pltpu.VMEM((seq_count, 2 * tokens), BF),
                pltpu.VMEM((columns, seq_count), BF),
                pltpu.SemaphoreType.DMA,
            ],
        ),
        compiler_params=params(48),
        cost_estimate=pl.CostEstimate(flops=1100000000, bytes_accessed=9000000, transcendentals=0),
    )(
        vit_mine,
        vit_theirs,
        audio_tokens,
        audio_theirs,
        weights.reshape(nz, nx, rows_w, columns),
        weights.reshape(nz, nx, rows_w, columns),
        places,
        text,
    )
    return result.T[:, None, :]


def solution(mesh):
    grid = Mesh(mesh.devices.reshape(4, 16, 4, 2), ("x", "z", "y", "core"))
    placed = (
        P(TM, None),
        P(None, MP),
        P(TM, MP),
        P(None, MP),
        P(MP, None),
        P(TM, MP),
        P(TM, MP),
        P(None, TM, MP),
        P(),
        P(),
        P(),
        P(),
    )
    return jax.shard_map(
        local, mesh=grid, in_specs=placed, out_specs=P(None, TM, MP), check_vma=False
    )
```

```python
import jax
import jax.numpy as jnp
from jax import lax
from jax.experimental import pallas as pl
from jax.experimental.pallas import tpu as pltpu
from jax.sharding import Mesh, PartitionSpec as P

AT = 50
VT = 64
BF = jnp.bfloat16
F32 = jnp.float32
I32 = jnp.int32
TM = ("x", "z")
MP = ("y", "core")
PAD_A = 32
VMEM = pl.BlockSpec(memory_space=pltpu.VMEM)
SMEM = pl.BlockSpec(memory_space=pltpu.SMEM)
ANY = pl.BlockSpec(memory_space=pl.ANY)
ROOT_HALF = 0.7071067811865476


def span_starts(span_order, offsets):
    listed = jnp.arange(span_order.shape[0], dtype=I32)
    matches = (span_order[:, None] == listed[None, :]).astype(I32)
    return jnp.sum(matches * offsets[:, None], axis=0)


def ring(value, axis, step):
    count = lax.axis_size(axis)
    return lax.ppermute(value, axis, [(i, (i + step) % count) for i in range(count)])


def swap(value):
    return lax.ppermute(value, "core", [(0, 1), (1, 0)])


def gelu(value):
    return 0.5 * value * (1.0 + lax.erf(value * ROOT_HALF))


def dot(a, b):
    return jnp.dot(a, b, preferred_element_type=F32)


def dot_nt(a, b):
    return lax.dot_general(a, b, (((1,), (1,)), ((), ())), preferred_element_type=F32)


def iota(shape, axis):
    return lax.broadcasted_iota(I32, shape, axis)


def params(mib):
    return pltpu.CompilerParams(vmem_limit_bytes=mib * 1024 * 1024)


def whole(shape):
    return pl.BlockSpec(shape, lambda *i: (0,) * len(shape))


def one_hot(condition):
    return jnp.where(condition, 1.0, 0.0).astype(BF)


def prep_kernel(
    order_ref, offset_ref, video_ref, patch_ref, mel_ref, rim_ref, conv_ref, out_ref, wide_mel, shifted
):
    rows, width = out_ref.shape
    spans, count = 3, patch_ref.shape[1]
    block = patch_ref.shape[0]
    nx, nz = lax.axis_size("x"), lax.axis_size("z")
    videos = nx * spans
    position = lax.axis_index("x") * lax.axis_size("z") + lax.axis_index("z")
    listed = iota(order_ref.shape, 1)

    def pick(condition, values):
        return jnp.sum(jnp.where(condition, values, 0), axis=1, keepdims=True)

    first = [pick(order_ref[...] == position * spans + k, offset_ref[...]) for k in range(spans)]
    kept = [pick(listed == position * spans + k, video_ref[...]) for k in range(spans)]
    patch = patch_ref[...]
    row = iota((rows, 1), 0)
    far, slot = row >> 4, row & 15
    to_x = sum((slot >= spans * i).astype(I32) for i in range(1, nx))
    is_video = slot < videos
    kind = jnp.where(is_video, slot - spans * to_x, slot - videos)

    def of_kind(values):
        return jnp.where(kind == 0, values[0], jnp.where(kind == 1, values[1], values[2]))

    start = of_kind(first)
    token = (kind << 6) + ((to_x * nz + far - start) & (VT - 1))
    target = jnp.where(is_video, token * 4, -8)
    frames = mel_ref.shape[0] // 4
    wide_mel[...] = mel_ref[...].astype(F32)
    f0, f1, f2, f3 = (wide_mel[pl.ds(k, frames, stride=4), :] for k in range(4))
    shifted[0:1, :] = rim_ref[...].astype(F32)
    shifted[1:frames, :] = wide_mel[pl.ds(3, frames - 1, stride=4), :]
    before, f0, f1, f2, f3 = (f.astype(BF) for f in (shifted[...], f0, f1, f2, f3))
    c0, c1, c2 = (conv_ref[:, k * 128 : (k + 1) * 128] for k in range(3))
    even = dot_nt(before, c0) + dot_nt(f0, c1) + dot_nt(f1, c2)
    odd = dot_nt(f1, c0) + dot_nt(f2, c1) + dot_nt(f3, c2)
    pooled = (0.5 * (gelu(even) + gelu(odd))).astype(BF)
    start = start + of_kind(kept)
    is_audio = (slot >= videos) & (kind < spans)
    patch_column, column = iota((rows, count), 1), iota((rows, frames), 1)
    for i in range(nx):
        index = jnp.minimum((i * nz + far - start) & (VT - 1), AT - 1) + kind * AT
        index = jnp.where(is_audio, index, -8)
        video = dot_nt(one_hot(patch_column == target + i), patch)
        audio = dot(one_hot(column == index), pooled)
        out_ref[:, i * block : (i + 1) * block] = (video + audio).astype(BF)


def vision_kernel(
    video_ref, audio_ref, up0, down0, up1, down1, send_ref, xs, wu, wd, sems
):
    copies = []
    for i, (u, d) in enumerate(((up0, down0), (up1, down1))):
        copies.append(pltpu.make_async_copy(u, wu.at[i], sems.at[2 * i]))
        copies.append(pltpu.make_async_copy(d, wd.at[i], sems.at[2 * i + 1]))
    for copy in copies:
        copy.start()
    ny, cores, half, width = video_ref.shape
    block = width // 4
    for y in range(ny):
        for c in range(cores):
            for s in range(4):
                a, b = (y * cores + c) * block, s * block
                xs[s * half : (s + 1) * half, a : a + block] = video_ref[y, c, :, b : b + block]
    wide = xs[...].astype(F32)
    centred = wide - jnp.mean(wide, axis=1, keepdims=True)
    spread = jnp.mean(centred * centred, axis=1, keepdims=True)
    normed = (centred * lax.rsqrt(spread + 1e-06)).astype(BF)
    total = None
    for i in range(2):
        copies[2 * i].wait()
        hidden = gelu(dot(normed, wu[i])).astype(BF)
        copies[2 * i + 1].wait()
        term = dot(hidden, wd[i])
        total = term if total is None else total + term
    total += wide * (1.0 / ny)
    parts = send_ref.shape[0] // 4
    some = half // parts
    send_ref[...] = jnp.zeros_like(send_ref)
    for s in range(4):
        for x in range(parts):
            a = s * half + x * some
            send_ref[x * ny + s, :some] = total[a : a + some].astype(BF)
            for c in range(cores):
                for k in range(3):
                    a, b = (c * 3 + k) * block, x * block
                    send_ref[x * ny + s, some:, a : a + block] = audio_ref[c, k, :, b : b + block]


def audio_kernel(in_ref, out_ref):
    ny, tokens, _ = out_ref.shape
    block, parts = in_ref.shape[2] // 8, in_ref.shape[0] // ny
    owners = tokens // 3
    near = owners // parts
    some = in_ref.shape[1] - near
    source, place = iota((block, 256), 0), iota((block, 256), 1)
    group = place // PAD_A
    lane = place - group * PAD_A
    spread = one_hot((lane < 20) & (source == group * 20 + lane))
    for y in range(ny):
        for c in range(2):
            for k in range(3):
                a = (c * 3 + k) * block
                rows = [in_ref[x * ny + y, some:, a : a + block] for x in range(parts)]
                piece = dot(jnp.concatenate(rows, axis=0), spread).astype(BF)
                out_ref[y, k * owners : (k + 1) * owners, c * 256 : (c + 1) * 256] = piece


def tail_kernel(
    own_ref,
    other_ref,
    audio_own_ref,
    audio_other_ref,
    weight_ref,
    place_ref,
    text_ref,
    out_ref,
    video,
    audio,
    spread,
    marks,
    text,
    sem,
):
    step = pl.program_id(0)
    fetch = pltpu.make_async_copy(text_ref, text, sem)

    @pl.when(step == 0)
    def _():
        fetch.start()
        video[...] = jnp.zeros_like(video)
        audio[...] = jnp.zeros_like(audio)
        spread[...] = jnp.zeros_like(spread)
        marks[...] = one_hot(place_ref[...] == iota(marks.shape, 0))

    nz, _, rows, columns = weight_ref.shape
    rows_a = rows // 5
    rows_m = rows - rows_a
    both = jnp.concatenate([own_ref[0], other_ref[0]], axis=0)
    video[...] += dot(both, weight_ref[:, 0, :rows_m, :].reshape(nz * rows_m, columns))
    for z in range(nz):
        spread[z * PAD_A : z * PAD_A + rows_a, :] = weight_ref[z, 0, rows_m:, :]
    tokens = jnp.concatenate([audio_own_ref[0], audio_other_ref[0]], axis=0)
    audio[...] += dot(tokens, spread[...])

    @pl.when(step == 3)
    def _():
        media = jnp.concatenate([video[...], audio[...]], axis=0).astype(BF)
        placed = lax.dot_general(
            media, marks[...], (((0,), (1,)), ((), ())), preferred_element_type=F32
        )
        taken = dot_nt(jnp.ones((8, media.shape[0]), BF), marks[...])[0:1, :]
        fetch.wait()
        out_ref[...] = jnp.where(taken > 0.5, placed, text[...].astype(F32)).astype(BF)


def local(
    mel_frames,
    conv_weight,
    patches,
    vit_up,
    vit_down,
    audio_proj,
    merger,
    text_rows,
    span_order,
    offsets,
    audio_count,
    video_count,
):
    nx, nz, ny = (lax.axis_size(a) for a in ("x", "z", "y"))
    owners = nx * nz
    position = lax.axis_index(TM)
    my_core = lax.axis_index("core")
    spans = mel_frames.shape[0] // (4 * AT)
    tokens = spans * owners
    half = tokens // 2
    columns, rows_m, rows_a = merger.shape[1], merger.shape[0], audio_proj.shape[0]
    rows_w = rows_m + rows_a
    width = 4 * patches.shape[1]
    full = vit_down.shape[1]

    rim = lax.ppermute(mel_frames[-1:], TM, [(i, i + 1) for i in range(owners - 1)])

    own = jnp.concatenate([merger, audio_proj], axis=0)
    everywhere = jnp.stack([own] * nx)
    rim, everywhere = lax.optimization_barrier((rim, everywhere))
    block = lax.all_to_all(everywhere, "x", 0, 0, tiled=True)

    starts = span_starts(span_order, offsets)
    prep_in = (
        span_order.reshape(1, -1),
        offsets.reshape(1, -1),
        video_count.reshape(1, -1),
        patches.T,
        mel_frames,
        rim,
        conv_weight.T,
    )
    outgoing = pl.pallas_call(
        prep_kernel,
        name="prep",
        out_shape=jax.ShapeDtypeStruct((nz * 16, width), BF),
        grid=(1,),
        in_specs=[whole(v.shape) for v in prep_in],
        out_specs=whole((nz * 16, width)),
        scratch_shapes=[
            pltpu.VMEM(mel_frames.shape, F32),
            pltpu.VMEM((spans * AT, mel_frames.shape[1]), F32),
        ],
        compiler_params=params(60),
        cost_estimate=pl.CostEstimate(
            flops=2000000000, bytes_accessed=8000000, transcendentals=500000
        ),
    )(*prep_in)
    block, outgoing = lax.optimization_barrier((block, outgoing))
    weights = lax.all_gather(block, "z", axis=0, tiled=False)
    arrived = lax.all_to_all(outgoing.reshape(nz, 16, width), "z", 0, 0, tiled=True)

    videos, half_z = nx * spans, nz // 2
    seq_count = text_rows.shape[0]
    video_where = jnp.mod(position - starts, owners)
    video_place = jnp.where(video_where < video_count, (starts + video_where) // owners, seq_count)
    audio_where = jnp.mod(position - starts - video_count, owners)
    audio_place = jnp.where(
        audio_where < audio_count, (starts + video_count + audio_where) // owners, seq_count
    )


    def ordered(places, axes):
        places = places.reshape(nx, 2, half_z, spans)
        places = jnp.where(my_core == 0, places, places[:, ::-1])
        return jnp.transpose(places, axes).reshape(-1)

    video_place = ordered(video_place, (1, 0, 2, 3))
    audio_place = ordered(audio_place, (1, 3, 0, 2))
    places = jnp.concatenate([video_place, audio_place])
    text = text_rows[:, 0, :].T

    arrived, places = lax.optimization_barrier((arrived, places.reshape(1, -1)))

    up_other, down_other = swap(vit_up), swap(vit_down)
    cores = lax.all_gather(arrived, "core", axis=0, tiled=False)
    near = lax.dynamic_slice_in_dim(cores, my_core * half_z, half_z, axis=1)
    pair = near[:, :, :videos].reshape(2, half_z, nx, spans, width)
    video_pair = jnp.transpose(pair, (0, 2, 1, 3, 4)).reshape(2, half, width)
    video_y = lax.all_gather(video_pair, "y", axis=0, tiled=False)
    audio_own = jnp.transpose(near[:, :, videos : videos + spans], (0, 2, 1, 3))

    some = half // nx
    rows_sent = some + half_z
    flops = 2 * 4 * half * full * 4 * vit_up.shape[1]
    partial_sum = pl.pallas_call(
        vision_kernel,
        name="vision",
        out_shape=jax.ShapeDtypeStruct((nx * ny, rows_sent, full), BF),
        in_specs=[VMEM, VMEM, ANY, ANY, ANY, ANY],
        out_specs=VMEM,
        scratch_shapes=[
            pltpu.VMEM((4 * half, full), BF),
            pltpu.VMEM((2,) + vit_up.shape, BF),
            pltpu.VMEM((2,) + vit_down.shape, BF),
            pltpu.SemaphoreType.DMA((4,)),
        ],
        compiler_params=params(28),
        cost_estimate=pl.CostEstimate(flops=flops, bytes_accessed=9000000, transcendentals=500000),
    )(video_y, audio_own, vit_up, vit_down, up_other, down_other)

    incoming = lax.all_to_all(partial_sum, ("x", "y"), 0, 0, tiled=True)
    audio_tokens = pl.pallas_call(
        audio_kernel,
        name="audio_spread",
        out_shape=jax.ShapeDtypeStruct((ny, half, nz * PAD_A), BF),
        in_specs=[VMEM],
        out_specs=VMEM,
        compiler_params=params(8),
    )(incoming)
    audio_theirs = swap(audio_tokens)
    summed = jnp.sum(incoming.reshape(nx, ny, rows_sent, full)[:, :, :some].astype(F32), axis=1)
    vit_out = summed.astype(BF).reshape(half, full)
    vit_mine = lax.all_gather(vit_out, "y", axis=0, tiled=False)
    vit_theirs = swap(vit_mine)

    result = pl.pallas_call(
        tail_kernel,
        name="project_place",
        out_shape=jax.ShapeDtypeStruct((columns, seq_count), BF),
        grid_spec=pl.GridSpec(
            grid=(nx,),
            in_specs=[
                pl.BlockSpec((1, half, full), lambda s: (s, 0, 0)),
                pl.BlockSpec((1, half, full), lambda s: (s, 0, 0)),
                pl.BlockSpec((1, half, nz * PAD_A), lambda s: (s, 0, 0)),
                pl.BlockSpec((1, half, nz * PAD_A), lambda s: (s, 0, 0)),
                pl.BlockSpec((nz, 1, rows_w, columns), lambda s: (0, s, 0, 0)),
                whole((1, 2 * tokens)),
                ANY,
            ],
            out_specs=whole((columns, seq_count)),
            scratch_shapes=[
                pltpu.VMEM((tokens, columns), F32),
                pltpu.VMEM((tokens, columns), F32),
                pltpu.VMEM((nz * PAD_A, columns), BF),
                pltpu.VMEM((seq_count, 2 * tokens), BF),
                pltpu.VMEM((columns, seq_count), BF),
                pltpu.SemaphoreType.DMA,
            ],
        ),
        compiler_params=params(48),
        cost_estimate=pl.CostEstimate(flops=1100000000, bytes_accessed=9000000, transcendentals=0),
    )(
        vit_mine,
        vit_theirs,
        audio_tokens,
        audio_theirs,
        weights.reshape(nz, nx, rows_w, columns),
        places,
        text,
    )
    return result.T[:, None, :]


def solution(mesh):
    grid = Mesh(mesh.devices.reshape(4, 16, 4, 2), ("x", "z", "y", "core"))
    placed = (
        P(TM, None),
        P(None, MP),
        P(TM, MP),
        P(None, MP),
        P(MP, None),
        P(TM, MP),
        P(TM, MP),
        P(None, TM, MP),
        P(),
        P(),
        P(),
        P(),
    )
    return jax.shard_map(
        local, mesh=grid, in_specs=placed, out_specs=P(None, TM, MP), check_vma=False
    )
```
